512 devices in a mesh: node: 32 (over y, x_hi, core), group: 16 (over z, x_lo).
Axes of the slice: x: 4 (x_hi: 2, x_lo: 2; x = x_hi * 2 + x_lo), y: 8, z: 8, core: 2. Of those that a mesh axis runs over, the one named last changes fastest.
Arguments:
- hidden_in: bfloat16 [98304, 8192], P(('node', 'group')), may hold values from -24 to 24
- key_grad: bfloat16 [98304, 512], P(('node', 'group')), may hold values from -0.19042969 to 0.19042969
- gain_second: bfloat16 [8192], P('group'), may hold values from 0.099609375 to 1.8984375
- weight_second: bfloat16 [8192, 512], P('group'), may hold values from -0.0625 to 0.0625
- weight_main: float32 [8192, 512], P(('node', 'group')), may hold values from -0.0625 to 0.0625
- weight_m: float32 [8192, 512], P(('node', 'group')), may hold values from -6 to 6
- weight_v: float32 [8192, 512], P(('node', 'group')), may hold values from 0.05 to 20
- gain_main: float32 [8192], P(('node', 'group')), may hold values from 0.5 to 1.5
- gain_m: float32 [8192], P(('node', 'group')), may hold values from -6 to 6
- gain_v: float32 [8192], P(('node', 'group')), may hold values from 0.05 to 20
Outputs:
- weight_main_new: float32 [8192, 512], P(('node', 'group'))
- weight_m_new: float32 [8192, 512], P(('node', 'group'))
- weight_v_new: float32 [8192, 512], P(('node', 'group'))
- gain_main_new: float32 [8192], P(('node', 'group'))
- gain_m_new: float32 [8192], P(('node', 'group'))
- gain_v_new: float32 [8192], P(('node', 'group'))
The draws below stay inside these ranges and needn't reach their ends.
All inputs are finite; a program needn't handle non-finite values.
Results may differ from the reference program's by a relative error of at most 0.0039.
Values may be sent and summed in bfloat16 or wider, within the bound.
No kernel may reach another device: no remote copies, remote signals or barrier semaphores. Data moves between devices by JAX's collectives and lax.ppermute only.
A program may use at most 128 MiB of HBM per device.

```python
import math
import jax
import jax.numpy as jnp
from jax import lax

D = 8192
HEADS = 4
HEAD = 128
TOK_DEV = 192
PROJ = 512
TOKENS = 98304
N_NODE = 32
N_GROUP = 16


def strengthened(array, key, source, target, parts, factor):
    def block_of(dim):
        return (jnp.arange(array.shape[dim]) // (array.shape[dim] // parts)).reshape((-1,) + (1,) * (array.ndim - 1 - dim))

    first = jax.random.permutation(key, parts)[block_of(target)]
    far = (block_of(target) + parts // 2) % parts
    return jnp.where((block_of(source) == first) | (block_of(source) == far), factor * array, array)


def levels(key, shape, pieces, low, largest):
    def one(dim, parts):
        draws = jax.random.uniform(jax.random.fold_in(jax.random.fold_in(key, 6), dim), (parts,), jnp.float32, low / len(pieces), largest / len(pieces))
        return jnp.repeat(jnp.exp(draws), shape[dim] // parts).reshape((-1,) + (1,) * (len(shape) - dim - 1))

    gain = one(*pieces[0])
    for cut in pieces[1:]:
        gain = gain * one(*cut)
    return gain


def normal_values(own_key, shape, spread, most, split=(), dtype=jnp.bfloat16):
    drawn = jax.random.normal(own_key, shape, jnp.float32) * spread
    if len(split) > 0:
        drawn = levels(own_key, shape, split, -0.22, 0.18) * drawn
    return jnp.clip(drawn, min=-most, max=most).astype(dtype)


def heavy_noise(stream_key, extent, spread, most, cuts, heavy, kind=jnp.bfloat16):
    entries = spread * jax.random.normal(stream_key, extent, jnp.float32)
    if cuts:
        entries = entries * levels(stream_key, extent, cuts, -0.22, 0.18)
    return jnp.clip(strengthened(entries, jax.random.fold_in(stream_key, 3), *heavy), -most, most).astype(kind)


def setup_inputs(seed: int = 0) -> dict:
    key_of = jax.random.split(jax.random.key(seed), 11)
    return {
        "hidden_in": heavy_noise(key_of[0], (TOKENS, D), 1.0, 24.0, ((0, 512),), (0, 1, 512, 6.0)),
        "key_grad": normal_values(key_of[1], (TOKENS, PROJ), (10.0 * TOKENS ** -0.5), 0.19042969, ((0, 512),)),
        "gain_second": jnp.clip(1.0 + 0.18 * jax.random.normal(key_of[2], (D,), jnp.float32), 0.099609375, 1.8984375).astype(jnp.bfloat16),
        "weight_second": normal_values(key_of[3], (D, PROJ), D ** -0.5, 0.0625, ((0, 16),)),
        "weight_main": normal_values(key_of[4], (D, PROJ), D ** -0.5, 0.0625, ((0, 512),), jnp.float32),
        "weight_m": normal_values(key_of[5], (D, PROJ), 1.0, 6.0, ((0, 512),), jnp.float32),
        "weight_v": jnp.clip(jnp.exp(math.log(20.0) - 5.9914645 * jax.random.uniform(key_of[6], (D, PROJ), jnp.float32) ** levels(key_of[6], (D, PROJ), ((0, 512),), -0.2, 0.2)), 0.05, 20.0),
        "gain_main": jnp.clip(1.0 + 0.1 * jax.random.normal(key_of[7], (D,), jnp.float32), 0.5, 1.5),
        "gain_m": normal_values(key_of[8], (D,), 1.0, 6.0, ((0, 512),), jnp.float32),
        "gain_v": jnp.clip(jnp.exp(math.log(20.0) - 5.9914645 * jax.random.uniform(key_of[9], (D,), jnp.float32) ** levels(key_of[9], (D,), ((0, 512),), -0.2, 0.2)), 0.05, 20.0),
    }


norm_eps = 1e-05
beta_one = 0.9
beta_two = 0.999
adam_eps = 1e-08
learn_rate = 0.0003
weight_decay = 0.1
bias_one = 1.0 - 2.6561398887587544e-05
bias_two = 1.0 - 0.9047921471137096

def rounded(values):
    return lax.optimization_barrier(values.astype(jnp.bfloat16)).astype(jnp.float32)

def adam_update(weights, moment_one, moment_two, gradient):
    moment_new = beta_one * moment_one + (1.0 - beta_one) * gradient
    square_new = beta_two * moment_two + (1.0 - beta_two) * gradient * gradient
    direction = moment_new / bias_one / (jnp.sqrt(square_new / bias_two) + adam_eps)
    return (weights - learn_rate * (direction + weight_decay * weights), moment_new, square_new)

def reference(hidden_in, key_grad, gain_second, weight_second, weight_main, weight_m, weight_v, gain_main, gain_m, gain_v):
    proj_width = HEADS * HEAD
    hidden_blocks = hidden_in.reshape(N_NODE, N_GROUP, TOK_DEV, D)
    key_blocks = key_grad.reshape(N_NODE, N_GROUP, TOK_DEV, proj_width)
    gain_wide = gain_second.astype(jnp.float32)

    def device_block(running, blocks):
        group_sum, gain_sum = running
        hidden_rows, key_rows = blocks
        wide_in = hidden_rows.astype(jnp.float32)
        inverse = lax.rsqrt(lax.optimization_barrier(jnp.mean(wide_in * wide_in, axis=1, keepdims=True)) + norm_eps)
        scaled = wide_in * inverse
        normed = (scaled * gain_wide).astype(jnp.bfloat16)
        partial_value = lax.dot_general(normed, key_rows, (((0,), (0,)), ((), ())), preferred_element_type=jnp.float32)
        input_grad = lax.dot_general(key_rows, weight_second, (((1,), (1,)), ((), ())), preferred_element_type=jnp.float32).astype(jnp.bfloat16)
        gain_term = lax.optimization_barrier(jnp.sum(input_grad.astype(jnp.float32) * scaled, axis=0))
        return ((group_sum + rounded(partial_value), gain_sum + gain_term), None)

    def node_block(running, blocks):
        weight_sum, gain_sum = running
        begin = (jnp.zeros((D, proj_width), jnp.float32), gain_sum)
        (group_sum, gain_sum), unused = lax.scan(device_block, begin, blocks)
        return ((weight_sum + rounded(group_sum), gain_sum), None)
    begin = (jnp.zeros((D, proj_width), jnp.float32), jnp.zeros((D,), jnp.float32))
    (weight_grad, gain_grad), unused = lax.scan(node_block, begin, (hidden_blocks, key_blocks))
    weight_new, weight_first, weight_square = adam_update(weight_main, weight_m, weight_v, weight_grad)
    gain_new, gain_first, gain_square = adam_update(gain_main, gain_m, gain_v, gain_grad)
    return (weight_new, weight_first, weight_square, gain_new, gain_first, gain_square)
```

```python
import jax
import jax.numpy as jnp
from jax import lax
from jax.experimental import pallas as pl
from jax.experimental.pallas import tpu as pltpu
from jax.sharding import Mesh, PartitionSpec as P

norm_eps = 1e-05
beta_one = 0.9
beta_two = 0.999
adam_eps = 1e-08
learn_rate = 0.0003
weight_decay = 0.1
bias_one = 1.0 - 2.6561398887587544e-05
bias_two = 1.0 - 0.9047921471137096

SIZES = (8, 2, 2, 8, 2)
ALL = ("y", "xh", "core", "z", "xl")
GROUP = ("z", "xl")
X = ("xh", "xl")
WIDE, NARROW = 256, 128


def adam_update(weights, moment_one, moment_two, gradient):
    moment_new = beta_one * moment_one + (1.0 - beta_one) * gradient
    square_new = beta_two * moment_two + (1.0 - beta_two) * gradient * gradient
    direction = moment_new / bias_one / (jnp.sqrt(square_new / bias_two) + adam_eps)
    return (weights - learn_rate * (direction + weight_decay * weights), moment_new, square_new)


def partial_kernel(core_ref, own_ref, got_ref, own_key_ref, got_key_ref, a_ref, b_ref, c_ref, keys):
    step = pl.program_id(0)
    tokens, width = own_ref.shape

    @pl.when(step == 0)
    def _():
        for half, (rows, key) in enumerate(((own_ref, own_key_ref), (got_ref, got_key_ref))):
            def add(i, total):
                block = rows[:, pl.ds(pl.multiple_of(i * 512, 512), 512)].astype(jnp.float32)
                block = block * block
                return total + (block[:, :128] + block[:, 128:256]) + (block[:, 256:384] + block[:, 384:])

            total = lax.fori_loop(0, width // 512, add, jnp.zeros((tokens, 128), jnp.float32))
            mean = jnp.sum(total, axis=1, keepdims=True) * (1.0 / width)
            inverse = lax.rsqrt(mean + norm_eps)
            keys[half * tokens : (half + 1) * tokens, :] = (
                key[...].astype(jnp.float32) * inverse
            ).astype(jnp.bfloat16)

    for xh in range(2):
        start = pl.multiple_of(step * 1024 + xh * 512 + core_ref[0] * 256, 256)
        total = lax.dot_general(
            own_ref[:, pl.ds(start, 256)],
            keys[:tokens, :],
            (((0,), (0,)), ((), ())),
            preferred_element_type=jnp.float32,
        ) + lax.dot_general(
            got_ref[:, pl.ds(start, 256)],
            keys[tokens:, :],
            (((0,), (0,)), ((), ())),
            preferred_element_type=jnp.float32,
        )
        rounded = total.astype(jnp.bfloat16).reshape(8, 2, 16, 512)
        for xl in range(2):
            a_ref[xh, xl, 0] = rounded[:, xl, :, :WIDE]
        b_ref[0, xh] = rounded[:, :, :, WIDE : WIDE + NARROW]
        c_ref[:, 0, xh] = rounded[:, :, :, WIDE + NARROW :]


def partial_grad(core, own, got, own_key, got_key):
    whole = lambda shape: pl.BlockSpec(shape, lambda i, c: (0, 0))
    return pl.pallas_call(
        partial_kernel,
        grid_spec=pltpu.PrefetchScalarGridSpec(
            num_scalar_prefetch=1,
            grid=(8,),
            in_specs=[whole(own.shape), whole(got.shape), whole(own_key.shape), whole(got_key.shape)],
            out_specs=[
                pl.BlockSpec((2, 2, 1, 8, 16, WIDE), lambda i, c: (0, 0, i, 0, 0, 0)),
                pl.BlockSpec((1, 2, 8, 2, 16, NARROW), lambda i, c: (i, 0, 0, 0, 0, 0)),
                pl.BlockSpec((8, 1, 2, 2, 16, NARROW), lambda i, c: (0, i, 0, 0, 0, 0)),
            ],
            scratch_shapes=[pltpu.VMEM((2 * own.shape[0], own_key.shape[1]), jnp.bfloat16)],
        ),
        out_shape=[
            jax.ShapeDtypeStruct((2, 2, 8, 8, 16, WIDE), jnp.bfloat16),
            jax.ShapeDtypeStruct((8, 2, 8, 2, 16, NARROW), jnp.bfloat16),
            jax.ShapeDtypeStruct((8, 8, 2, 2, 16, NARROW), jnp.bfloat16),
        ],
        compiler_params=pltpu.CompilerParams(vmem_limit_bytes=40 * 1024 * 1024),
        cost_estimate=pl.CostEstimate(
            flops=2 * 384 * 4096 * 512, bytes_accessed=11 * 1024 * 1024, transcendentals=0
        ),
    )(core, own, got, own_key, got_key)


def exchange(value, axes):
    return lax.all_to_all(value, axes, split_axis=0, concat_axis=0, tiled=True)


def summed(value):
    return jnp.sum(value.astype(jnp.float32), axis=0)


def on_device(
    hidden_in,
    key_grad,
    gain_second,
    weight_second,
    weight_main,
    weight_m,
    weight_v,
    gain_main,
    gain_m,
    gain_v,
):
    swap = [(0, 1), (1, 0)]
    got = lax.ppermute(hidden_in, "core", swap)
    got_key = lax.ppermute(key_grad, "core", swap)

    node = lax.axis_index(("y", "xh", "core"))
    rows = lax.dynamic_slice_in_dim(weight_second, node * 16, 16, 0)
    gains = lax.dynamic_slice_in_dim(gain_second, node * 16, 16, 0)
    pairs = [
        (m * 16 + g, (2 * g + m // 16) * 16 + m % 16) for m in range(32) for g in range(16)
    ]
    packed = jnp.concatenate([rows, jnp.broadcast_to(gains[:, None], (16, 128))], axis=1)
    packed = lax.ppermute(packed, ALL, pairs).astype(jnp.float32)
    rows, gains = packed[:, :512], packed[:, 512:513]

    core = lax.axis_index("core").astype(jnp.int32).reshape(1)
    wide, left, right = partial_grad(core, hidden_in, got, key_grad, got_key)
    wide = exchange(wide.reshape(4, 64, 16, WIDE), X)
    left = exchange(left.reshape(8, 32, 16, NARROW), "y")
    right = exchange(right.reshape(8, 32, 16, NARROW), "z")
    wide, left, right = (summed(v).astype(jnp.bfloat16) for v in (wide, left, right))
    wide = exchange(wide, ("y", "z"))
    left = exchange(left, ("xh", "z", "xl"))
    right = exchange(right, ("y", "xh", "xl"))
    scaled_grad = jnp.concatenate([summed(wide), summed(left), summed(right)], axis=1)

    weight_grad = scaled_grad * gains
    gain_grad = jnp.sum(scaled_grad * rows, axis=1)
    weight_new, weight_first, weight_square = adam_update(
        weight_main, weight_m, weight_v, weight_grad
    )
    gain_new, gain_first, gain_square = adam_update(gain_main, gain_m, gain_v, gain_grad)
    return (weight_new, weight_first, weight_square, gain_new, gain_first, gain_square)


def solution(mesh):
    fine = Mesh(mesh.devices.reshape(SIZES), ALL)
    placed = (
        P(ALL, None),
        P(ALL, None),
        P(GROUP),
        P(GROUP, None),
        P(ALL, None),
        P(ALL, None),
        P(ALL, None),
        P(ALL),
        P(ALL),
        P(ALL),
    )
    return jax.shard_map(
        on_device,
        mesh=fine,
        in_specs=placed,
        out_specs=(P(ALL, None),) * 3 + (P(ALL),) * 3,
        check_vma=False,
    )
```

```python
import jax
import jax.numpy as jnp
from jax import lax
from jax.experimental import pallas as pl
from jax.experimental.pallas import tpu as pltpu
from jax.sharding import Mesh, PartitionSpec as P

norm_eps = 1e-05
beta_one = 0.9
beta_two = 0.999
adam_eps = 1e-08
learn_rate = 0.0003
weight_decay = 0.1
bias_one = 1.0 - 2.6561398887587544e-05
bias_two = 1.0 - 0.9047921471137096

SIZES = (4, 2, 2, 2, 4, 2, 2)
ALL = ("yh", "yl", "xh", "core", "zh", "zl", "xl")
NODE, GROUP = ALL[:4], ALL[4:]
NEAR, FAR = ("yl", "xh", "zl", "xl"), ("yh", "zh")


def adam_update(weights, moment_one, moment_two, gradient):
    moment_new = beta_one * moment_one + (1.0 - beta_one) * gradient
    square_new = beta_two * moment_two + (1.0 - beta_two) * gradient * gradient
    direction = moment_new / bias_one / (jnp.sqrt(square_new / bias_two) + adam_eps)
    return (weights - learn_rate * (direction + weight_decay * weights), moment_new, square_new)


def partial_kernel(core_ref, own_ref, got_ref, own_key_ref, got_key_ref, out_ref, keys):
    step = pl.program_id(0)
    tokens, width = own_ref.shape

    @pl.when(step == 0)
    def _():
        for half, (rows, key) in enumerate(((own_ref, own_key_ref), (got_ref, got_key_ref))):
            def add(i, total):
                block = rows[:, pl.ds(pl.multiple_of(i * 512, 512), 512)].astype(jnp.float32)
                block = block * block
                return total + (block[:, :128] + block[:, 128:256]) + (block[:, 256:384] + block[:, 384:])

            total = lax.fori_loop(0, width // 512, add, jnp.zeros((tokens, 128), jnp.float32))
            mean = jnp.sum(total, axis=1, keepdims=True) * (1.0 / width)
            inverse = lax.rsqrt(mean + norm_eps)
            keys[half * tokens : (half + 1) * tokens, :] = (
                key[...].astype(jnp.float32) * inverse
            ).astype(jnp.bfloat16)

    for xh in range(2):
        start = pl.multiple_of(step * 1024 + xh * 512 + core_ref[0] * 256, 256)
        total = lax.dot_general(
            own_ref[:, pl.ds(start, 256)],
            keys[:tokens, :],
            (((0,), (0,)), ((), ())),
            preferred_element_type=jnp.float32,
        ) + lax.dot_general(
            got_ref[:, pl.ds(start, 256)],
            keys[tokens:, :],
            (((0,), (0,)), ((), ())),
            preferred_element_type=jnp.float32,
        )
        rounded = total.astype(jnp.bfloat16).reshape(4, 2, 2, 16, 512)
        for zl in range(2):
            for xl in range(2):
                out_ref[0, xh, zl, xl, 0] = rounded[:, zl, xl]


def partial_grad(core, own, got, own_key, got_key):
    whole = lambda shape: pl.BlockSpec(shape, lambda i, c: (0, 0))
    return pl.pallas_call(
        partial_kernel,
        grid_spec=pltpu.PrefetchScalarGridSpec(
            num_scalar_prefetch=1,
            grid=(8,),
            in_specs=[whole(own.shape), whole(got.shape), whole(own_key.shape), whole(got_key.shape)],
            out_specs=pl.BlockSpec(
                (1, 2, 2, 2, 1, 4, 16, 512), lambda i, c: (i % 2, 0, 0, 0, i // 2, 0, 0, 0)
            ),
            scratch_shapes=[pltpu.VMEM((2 * own.shape[0], own_key.shape[1]), jnp.bfloat16)],
        ),
        out_shape=jax.ShapeDtypeStruct((2, 2, 2, 2, 4, 4, 16, 512), jnp.bfloat16),
        compiler_params=pltpu.CompilerParams(vmem_limit_bytes=40 * 1024 * 1024),
        cost_estimate=pl.CostEstimate(
            flops=2 * 384 * 4096 * 512, bytes_accessed=11 * 1024 * 1024, transcendentals=0
        ),
    )(core, own, got, own_key, got_key)


def exchange(value, axes):
    return lax.all_to_all(value, axes, split_axis=0, concat_axis=0, tiled=True)


def summed(value):
    return jnp.sum(value.astype(jnp.float32), axis=0)


def on_device(
    hidden_in,
    key_grad,
    gain_second,
    weight_second,
    weight_main,
    weight_m,
    weight_v,
    gain_main,
    gain_m,
    gain_v,
):
    swap = [(0, 1), (1, 0)]
    got = lax.ppermute(hidden_in, "core", swap)
    got_key = lax.ppermute(key_grad, "core", swap)

    node = lax.axis_index(NODE)
    rows = lax.dynamic_slice_in_dim(weight_second, node * 16, 16, 0)
    gains = lax.dynamic_slice_in_dim(gain_second, node * 16, 16, 0)
    pairs = [
        (m * 16 + g, (2 * g + m // 16) * 16 + m % 16) for m in range(32) for g in range(16)
    ]
    packed = jnp.concatenate([rows, jnp.broadcast_to(gains[:, None], (16, 128))], axis=1)
    packed = lax.ppermute(packed, ALL, pairs).astype(jnp.float32)
    rows, gains = packed[:, :512], packed[:, 512:513]

    core = lax.axis_index("core").astype(jnp.int32).reshape(1)
    partial_value = partial_grad(core, hidden_in, got, key_grad, got_key)
    near = exchange(partial_value.reshape(16, 16, 16, 512), NEAR)
    far = exchange(summed(near).astype(jnp.bfloat16), FAR)
    scaled_grad = summed(far)

    weight_grad = scaled_grad * gains
    gain_grad = jnp.sum(scaled_grad * rows, axis=1)
    weight_new, weight_first, weight_square = adam_update(
        weight_main, weight_m, weight_v, weight_grad
    )
    gain_new, gain_first, gain_square = adam_update(gain_main, gain_m, gain_v, gain_grad)
    return (weight_new, weight_first, weight_square, gain_new, gain_first, gain_square)


def solution(mesh):
    fine = Mesh(mesh.devices.reshape(SIZES), ALL)
    placed = (
        P(ALL, None),
        P(ALL, None),
        P(GROUP),
        P(GROUP, None),
        P(ALL, None),
        P(ALL, None),
        P(ALL, None),
        P(ALL),
        P(ALL),
        P(ALL),
    )
    return jax.shard_map(
        on_device,
        mesh=fine,
        in_specs=placed,
        out_specs=(P(ALL, None),) * 3 + (P(ALL),) * 3,
        check_vma=False,
    )
```

```python
import jax
import jax.numpy as jnp
from jax import lax
from jax.experimental import pallas as pl
from jax.experimental.pallas import tpu as pltpu
from jax.sharding import Mesh, PartitionSpec as P

norm_eps = 1e-05
beta_one = 0.9
beta_two = 0.999
adam_eps = 1e-08
learn_rate = 0.0003
weight_decay = 0.1
bias_one = 1.0 - 2.6561398887587544e-05
bias_two = 1.0 - 0.9047921471137096

SIZES = (4, 2, 2, 2, 4, 2, 2)
ALL = ("yh", "yl", "xh", "core", "zh", "zl", "xl")
NODE, GROUP = ALL[:4], ALL[4:]
FAR = ("yh", "xh", "zh")


def near_groups():
    groups = []
    for core in range(2):
        for ky in range(core, 8, 2):
            for kx in range(core, 4, 2):
                for kz in range(core, 8, 2):
                    members = []
                    for yl in range(2):
                        for xl in range(2):
                            for zl in range(2):
                                y = (ky + (yl != core)) % 8
                                x = (kx + (xl != core)) % 4
                                z = (kz + (zl != core)) % 8
                                members.append((((y * 2 + x // 2) * 2 + core) * 8 + z) * 2 + x % 2)
                    groups.append(members)
    return groups


def adam_update(weights, moment_one, moment_two, gradient):
    moment_new = beta_one * moment_one + (1.0 - beta_one) * gradient
    square_new = beta_two * moment_two + (1.0 - beta_two) * gradient * gradient
    direction = moment_new / bias_one / (jnp.sqrt(square_new / bias_two) + adam_eps)
    return (weights - learn_rate * (direction + weight_decay * weights), moment_new, square_new)


def partial_kernel(core_ref, own_ref, got_ref, own_key_ref, got_key_ref, out_ref, keys):
    step = pl.program_id(0)
    tokens, width = own_ref.shape

    @pl.when(step == 0)
    def _():
        for half, (rows, key) in enumerate(((own_ref, own_key_ref), (got_ref, got_key_ref))):
            def add(i, total):
                block = rows[:, pl.ds(pl.multiple_of(i * 512, 512), 512)].astype(jnp.float32)
                block = block * block
                return total + (block[:, :128] + block[:, 128:256]) + (block[:, 256:384] + block[:, 384:])

            total = lax.fori_loop(0, width // 512, add, jnp.zeros((tokens, 128), jnp.float32))
            mean = jnp.sum(total, axis=1, keepdims=True) * (1.0 / width)
            inverse = lax.rsqrt(mean + norm_eps)
            keys[half * tokens : (half + 1) * tokens, :] = (
                key[...].astype(jnp.float32) * inverse
            ).astype(jnp.bfloat16)

    for xh in range(2):
        start = pl.multiple_of(step * 1024 + xh * 512 + core_ref[0] * 256, 256)
        total = lax.dot_general(
            own_ref[:, pl.ds(start, 256)],
            keys[:tokens, :],
            (((0,), (0,)), ((), ())),
            preferred_element_type=jnp.float32,
        ) + lax.dot_general(
            got_ref[:, pl.ds(start, 256)],
            keys[tokens:, :],
            (((0,), (0,)), ((), ())),
            preferred_element_type=jnp.float32,
        )
        rounded = total.astype(jnp.bfloat16).reshape(4, 2, 2, 16, 512)
        for zl in range(2):
            for xl in range(2):
                out_ref[0, xl, zl, 0, xh] = rounded[:, zl, xl]


def partial_grad(core, own, got, own_key, got_key):
    whole = lambda shape: pl.BlockSpec(shape, lambda i, c: (0, 0))
    return pl.pallas_call(
        partial_kernel,
        grid_spec=pltpu.PrefetchScalarGridSpec(
            num_scalar_prefetch=1,
            grid=(8,),
            in_specs=[whole(own.shape), whole(got.shape), whole(own_key.shape), whole(got_key.shape)],
            out_specs=pl.BlockSpec(
                (1, 2, 2, 1, 2, 4, 16, 512), lambda i, c: (i % 2, 0, 0, i // 2, 0, 0, 0, 0)
            ),
            scratch_shapes=[pltpu.VMEM((2 * own.shape[0], own_key.shape[1]), jnp.bfloat16)],
        ),
        out_shape=jax.ShapeDtypeStruct((2, 2, 2, 4, 2, 4, 16, 512), jnp.bfloat16),
        compiler_params=pltpu.CompilerParams(vmem_limit_bytes=40 * 1024 * 1024),
        cost_estimate=pl.CostEstimate(
            flops=2 * 384 * 4096 * 512, bytes_accessed=11 * 1024 * 1024, transcendentals=0
        ),
    )(core, own, got, own_key, got_key)


def exchange(value, axes, groups=None):
    return lax.all_to_all(
        value, axes, split_axis=0, concat_axis=0, axis_index_groups=groups, tiled=True
    )


def summed(value):
    return jnp.sum(value.astype(jnp.float32), axis=0)


def on_device(
    hidden_in,
    key_grad,
    gain_second,
    weight_second,
    weight_main,
    weight_m,
    weight_v,
    gain_main,
    gain_m,
    gain_v,
):
    swap = [(0, 1), (1, 0)]
    got = lax.ppermute(hidden_in, "core", swap)
    got_key = lax.ppermute(key_grad, "core", swap)

    node = lax.axis_index(NODE)
    rows = lax.dynamic_slice_in_dim(weight_second, node * 16, 16, 0)
    gains = lax.dynamic_slice_in_dim(gain_second, node * 16, 16, 0)
    pairs = [
        (m * 16 + g, (2 * g + m // 16) * 16 + m % 16) for m in range(32) for g in range(16)
    ]
    packed = jnp.concatenate([rows, jnp.broadcast_to(gains[:, None], (16, 128))], axis=1)
    packed = lax.ppermute(packed, ALL, pairs).astype(jnp.float32)
    rows, gains = packed[:, :512], packed[:, 512:513]

    core = lax.axis_index("core").astype(jnp.int32).reshape(1)
    partial_value = partial_grad(core, hidden_in, got, key_grad, got_key)
    near = exchange(partial_value.reshape(8, 32, 16, 512), ALL, near_groups())
    far = exchange(summed(near).astype(jnp.bfloat16), FAR)
    scaled_grad = summed(far)

    weight_grad = scaled_grad * gains
    gain_grad = jnp.sum(scaled_grad * rows, axis=1)
    weight_new, weight_first, weight_square = adam_update(
        weight_main, weight_m, weight_v, weight_grad
    )
    gain_new, gain_first, gain_square = adam_update(gain_main, gain_m, gain_v, gain_grad)
    return (weight_new, weight_first, weight_square, gain_new, gain_first, gain_square)


def solution(mesh):
    fine = Mesh(mesh.devices.reshape(SIZES), ALL)
    placed = (
        P(ALL, None),
        P(ALL, None),
        P(GROUP),
        P(GROUP, None),
        P(ALL, None),
        P(ALL, None),
        P(ALL, None),
        P(ALL),
        P(ALL),
        P(ALL),
    )
    return jax.shard_map(
        on_device,
        mesh=fine,
        in_specs=placed,
        out_specs=(P(ALL, None),) * 3 + (P(ALL),) * 3,
        check_vma=False,
    )
```

```python
import jax
import jax.numpy as jnp
from jax import lax
from jax.experimental import pallas as pl
from jax.experimental.pallas import tpu as pltpu
from jax.sharding import Mesh, PartitionSpec as P

norm_eps = 1e-05
beta_one = 0.9
beta_two = 0.999
adam_eps = 1e-08
learn_rate = 0.0003
weight_decay = 0.1
bias_one = 1.0 - 2.6561398887587544e-05
bias_two = 1.0 - 0.9047921471137096

SIZES = (4, 2, 2, 2, 4, 2, 2)
ALL = ("yh", "yl", "xh", "core", "zh", "zl", "xl")
NODE, GROUP = ALL[:4], ALL[4:]
FAR = ("yh", "xh", "zh")


def near_groups():
    groups = []
    for core in range(2):
        for ky in range(core, 8, 2):
            for kx in range(core, 4, 2):
                for kz in range(core, 8, 2):
                    members = []
                    for yl in range(2):
                        for xl in range(2):
                            for zl in range(2):
                                y = (ky + (yl != core)) % 8
                                x = (kx + (xl != core)) % 4
                                z = (kz + (zl != core)) % 8
                                members.append((((y * 2 + x // 2) * 2 + core) * 8 + z) * 2 + x % 2)
                    groups.append(members)
    return groups


def adam_update(weights, moment_one, moment_two, gradient):
    moment_new = beta_one * moment_one + (1.0 - beta_one) * gradient
    square_new = beta_two * moment_two + (1.0 - beta_two) * gradient * gradient
    direction = moment_new / bias_one / (jnp.sqrt(square_new / bias_two) + adam_eps)
    return (weights - learn_rate * (direction + weight_decay * weights), moment_new, square_new)


PIECES = 4


def square_sums(ref, first, count, total):
    def add(i, total):
        block = ref[:, pl.ds(pl.multiple_of(first + i * 512, 512), 512)].astype(jnp.float32)
        block = block * block
        return total + (block[:, :128] + block[:, 128:256]) + (block[:, 256:384] + block[:, 384:])

    return lax.fori_loop(0, count // 512, add, total)


def normed_key(key_ref, total, width):
    mean = jnp.sum(total, axis=1, keepdims=True) * (1.0 / width)
    return (key_ref[...].astype(jnp.float32) * lax.rsqrt(mean + norm_eps)).astype(jnp.bfloat16)


def fetch(source, target, semaphores, piece):
    width = source.shape[1] // PIECES
    columns = pl.ds(piece * width, width)
    return pltpu.make_async_copy(
        source.at[:, columns], target.at[:, columns], semaphores.at[piece]
    )


def own_kernel(core_ref, own_ref, key_ref, half_ref, scaled_ref, own, semaphores):
    tokens, width = own.shape
    for piece in range(PIECES):
        fetch(own_ref, own, semaphores, piece).start()
    total = jnp.zeros((tokens, 128), jnp.float32)
    for piece in range(PIECES):
        fetch(own_ref, own, semaphores, piece).wait()
        total = square_sums(own, piece * (width // PIECES), width // PIECES, total)
        for k in range(piece * 4, piece * 4 + 4):
            start = pl.multiple_of(k * 512 + core_ref[0] * 256, 256)
            half_ref[:, k * 256 : k * 256 + 256] = own[:, pl.ds(start, 256)]
    scaled_ref[...] = normed_key(key_ref, total, width)


def pair_kernel(
    core_ref, half_ref, scaled_ref, got_ref, key_ref, out_ref, got, keys, out, semaphores, out_sems
):
    tokens, width = got.shape
    for piece in range(PIECES):
        fetch(got_ref, got, semaphores, piece).start()
    keys[:tokens, :] = scaled_ref[...]
    total = jnp.zeros((tokens, 128), jnp.float32)
    for piece in range(PIECES):
        fetch(got_ref, got, semaphores, piece).wait()
        total = square_sums(got, piece * (width // PIECES), width // PIECES, total)
    keys[tokens:, :] = normed_key(key_ref, total, width)

    def store(yh, yl):
        return pltpu.make_async_copy(
            out.at[yl, :, :, yh], out_ref.at[yl, :, :, yh], out_sems.at[yl, yh]
        )

    def step(yh, carry):
        for yl in range(2):
            for xh in range(2):
                start = (yh * 2 + yl) * 512 + xh * 256
                other = 2 * start + core_ref[0] * 256
                rows = jnp.concatenate(
                    [
                        half_ref[:, pl.ds(pl.multiple_of(start, 256), 256)],
                        got[:, pl.ds(pl.multiple_of(other, 256), 256)],
                    ],
                    axis=0,
                )
                product = lax.dot_general(
                    rows, keys[...], (((0,), (0,)), ((), ())), preferred_element_type=jnp.float32
                )
                product = product.astype(jnp.bfloat16).reshape(4, 2, 2, 16, 512)
                for zl in range(2):
                    for xl in range(2):
                        out[yl, xl, zl, yh, xh] = product[:, zl, xl]
            store(yh, yl).start()
        return carry

    lax.fori_loop(0, 4, step, 0)
    for yh in range(4):
        for yl in range(2):
            store(yh, yl).wait()


VMEM = pl.BlockSpec(memory_space=pltpu.MemorySpace.VMEM)
SMEM = pl.BlockSpec(memory_space=pltpu.MemorySpace.SMEM)
HBM = pl.BlockSpec(memory_space=pltpu.MemorySpace.HBM)


def own_part(core, own, key):
    tokens, width = own.shape
    return pl.pallas_call(
        own_kernel,
        in_specs=[SMEM, HBM, VMEM],
        out_specs=[VMEM, VMEM],
        out_shape=[
            jax.ShapeDtypeStruct((tokens, width // 2), jnp.bfloat16),
            jax.ShapeDtypeStruct(key.shape, jnp.bfloat16),
        ],
        scratch_shapes=[pltpu.VMEM(own.shape, jnp.bfloat16), pltpu.SemaphoreType.DMA((PIECES,))],
        compiler_params=pltpu.CompilerParams(vmem_limit_bytes=12 * 1024 * 1024),
        cost_estimate=pl.CostEstimate(
            flops=4 * tokens * width, bytes_accessed=5 * 1024 * 1024, transcendentals=0
        ),
    )(core, own, key)


def pair_partial(core, half, scaled, got, key):
    tokens, width = got.shape
    proj = key.shape[1]
    shape = (2, 2, 2, 4, 2, 4, 16, proj)
    return pl.pallas_call(
        pair_kernel,
        in_specs=[SMEM, VMEM, VMEM, HBM, VMEM],
        out_specs=HBM,
        out_shape=jax.ShapeDtypeStruct(shape, jnp.bfloat16),
        scratch_shapes=[
            pltpu.VMEM(got.shape, jnp.bfloat16),
            pltpu.VMEM((2 * tokens, proj), jnp.bfloat16),
            pltpu.VMEM(shape, jnp.bfloat16),
            pltpu.SemaphoreType.DMA((PIECES,)),
            pltpu.SemaphoreType.DMA((2, 4)),
        ],
        compiler_params=pltpu.CompilerParams(vmem_limit_bytes=48 * 1024 * 1024),
        cost_estimate=pl.CostEstimate(
            flops=2 * tokens * width * proj, bytes_accessed=9 * 1024 * 1024, transcendentals=0
        ),
    )(core, half, scaled, got, key)


def sum_kernel(value_ref, out_ref):
    total = value_ref[0].astype(jnp.float32)
    for source in range(1, value_ref.shape[0]):
        total = total + value_ref[source].astype(jnp.float32)
    out_ref[...] = total.astype(jnp.bfloat16)


def near_sum(value):
    sources, blocks, rows, proj = value.shape
    return pl.pallas_call(
        sum_kernel,
        grid=(4,),
        in_specs=[pl.BlockSpec((sources, blocks // 4, rows, proj), lambda i: (0, i, 0, 0))],
        out_specs=pl.BlockSpec((blocks // 4, rows, proj), lambda i: (i, 0, 0)),
        out_shape=jax.ShapeDtypeStruct((blocks, rows, proj), jnp.bfloat16),
        compiler_params=pltpu.CompilerParams(vmem_limit_bytes=16 * 1024 * 1024),
    )(value)


def exchange(value, axes, groups=None):
    return lax.all_to_all(
        value, axes, split_axis=0, concat_axis=0, axis_index_groups=groups, tiled=True
    )


def summed(value):
    return jnp.sum(value.astype(jnp.float32), axis=0)


def on_device(
    hidden_in,
    key_grad,
    gain_second,
    weight_second,
    weight_main,
    weight_m,
    weight_v,
    gain_main,
    gain_m,
    gain_v,
):
    swap = [(0, 1), (1, 0)]
    got = lax.ppermute(hidden_in, "core", swap)
    got_key = lax.ppermute(key_grad, "core", swap)

    node = lax.axis_index(NODE)
    rows = lax.dynamic_slice_in_dim(weight_second, node * 16, 16, 0)
    gains = lax.dynamic_slice_in_dim(gain_second, node * 16, 16, 0)
    pairs = [
        (m * 16 + g, (2 * g + m // 16) * 16 + m % 16) for m in range(32) for g in range(16)
    ]
    packed = jnp.concatenate([rows, jnp.broadcast_to(gains[:, None], (16, 128))], axis=1)
    packed = lax.ppermute(packed, ALL, pairs).astype(jnp.float32)

    core = lax.axis_index("core").astype(jnp.int32).reshape(1)
    half, scaled_key = own_part(core, hidden_in, key_grad)
    partial_value = pair_partial(core, half, scaled_key, got, got_key)
    near = exchange(partial_value.reshape(8, 32, 16, 512), ALL, near_groups())
    near, packed = lax.optimization_barrier((near, packed))
    rows, gains = packed[:, :512], packed[:, 512:513]
    scaled_grad = summed(exchange(near_sum(near), FAR))

    weight_grad = scaled_grad * gains
    gain_grad = jnp.sum(scaled_grad * rows, axis=1)
    weight_new, weight_first, weight_square = adam_update(
        weight_main, weight_m, weight_v, weight_grad
    )
    gain_new, gain_first, gain_square = adam_update(gain_main, gain_m, gain_v, gain_grad)
    return (weight_new, weight_first, weight_square, gain_new, gain_first, gain_square)


def solution(mesh):
    fine = Mesh(mesh.devices.reshape(SIZES), ALL)
    placed = (
        P(ALL, None),
        P(ALL, None),
        P(GROUP),
        P(GROUP, None),
        P(ALL, None),
        P(ALL, None),
        P(ALL, None),
        P(ALL),
        P(ALL),
        P(ALL),
    )
    return jax.shard_map(
        on_device,
        mesh=fine,
        in_specs=placed,
        out_specs=(P(ALL, None),) * 3 + (P(ALL),) * 3,
        check_vma=False,
    )
```

```python
import jax
import jax.numpy as jnp
from jax import lax
from jax.experimental import pallas as pl
from jax.experimental.pallas import tpu as pltpu
from jax.sharding import Mesh, PartitionSpec as P

norm_eps = 1e-05
beta_one = 0.9
beta_two = 0.999
adam_eps = 1e-08
learn_rate = 0.0003
weight_decay = 0.1
bias_one = 1.0 - 2.6561398887587544e-05
bias_two = 1.0 - 0.9047921471137096

SIZES = (4, 2, 2, 2, 4, 2, 2)
ALL = ("yh", "yl", "xh", "core", "zh", "zl", "xl")
NODE, GROUP = ALL[:4], ALL[4:]
FAR = ("yh", "xh", "zh")


def near_groups():
    groups = []
    for core in range(2):
        for ky in range(core, 8, 2):
            for kx in range(core, 4, 2):
                for kz in range(core, 8, 2):
                    members = []
                    for yl in range(2):
                        for xl in range(2):
                            for zl in range(2):
                                y = (ky + (yl != core)) % 8
                                x = (kx + (xl != core)) % 4
                                z = (kz + (zl != core)) % 8
                                members.append((((y * 2 + x // 2) * 2 + core) * 8 + z) * 2 + x % 2)
                    groups.append(members)
    return groups


def adam_update(weights, moment_one, moment_two, gradient):
    moment_new = beta_one * moment_one + (1.0 - beta_one) * gradient
    square_new = beta_two * moment_two + (1.0 - beta_two) * gradient * gradient
    direction = moment_new / bias_one / (jnp.sqrt(square_new / bias_two) + adam_eps)
    return (weights - learn_rate * (direction + weight_decay * weights), moment_new, square_new)


PIECES = 4


def own_kernel(
    core_ref,
    own_ref,
    key_ref,
    send_ref,
    kept_ref,
    scaled_ref,
    own,
    key,
    send,
    own_sems,
    send_sems,
):
    tokens, width = own.shape
    kept = width // 2
    part = width // PIECES

    def fetch(piece):
        columns = pl.ds(piece * part, part)
        return pltpu.make_async_copy(
            own_ref.at[:, columns], own.at[:, columns], own_sems.at[piece]
        )

    def store(piece):
        start = piece * (part // 2)
        columns = pl.ds(start, part // 2 if piece < PIECES else send.shape[1] - start)
        return pltpu.make_async_copy(
            send.at[:, columns], send_ref.at[:, columns], send_sems.at[piece]
        )

    fetch_key = pltpu.make_async_copy(key_ref, key, own_sems.at[PIECES])
    for piece in range(PIECES):
        fetch(piece).start()
    fetch_key.start()
    total = jnp.zeros((tokens, 128), jnp.float32)
    for piece in range(PIECES):
        fetch(piece).wait()

        def add(i, total):
            block = own[:, pl.ds(pl.multiple_of(piece * part + i * 512, 512), 512)]
            block = block.astype(jnp.float32)
            block = block * block
            return (
                total
                + (block[:, :128] + block[:, 128:256])
                + (block[:, 256:384] + block[:, 384:])
            )

        total = lax.fori_loop(0, part // 512, add, total)
        for k in range(piece * part // 512, (piece + 1) * part // 512):
            columns = slice(k * 256, k * 256 + 256)
            start = pl.multiple_of(k * 512 + (1 - core_ref[0]) * 256, 256)
            send[:, columns] = own[:, pl.ds(start, 256)]
            start = pl.multiple_of(k * 512 + core_ref[0] * 256, 256)
            kept_ref[:, columns] = own[:, pl.ds(start, 256)]
        store(piece).start()
    mean = jnp.sum(total, axis=1, keepdims=True) * (1.0 / width)
    fetch_key.wait()
    scaled = key[...].astype(jnp.float32) * lax.rsqrt(mean + norm_eps)
    scaled_ref[...] = scaled.astype(jnp.bfloat16)
    send[:, kept:] = scaled_ref[...]
    store(PIECES).start()
    for piece in range(PIECES + 1):
        store(piece).wait()


def pair_kernel(kept_ref, scaled_ref, got_ref, out_ref, keys, out, out_sems):
    tokens, kept = kept_ref.shape

    def store(yh, yl):
        return pltpu.make_async_copy(
            out.at[yl, :, :, yh], out_ref.at[yl, :, :, yh], out_sems.at[yl, yh]
        )

    keys[:tokens, :] = scaled_ref[...]
    keys[tokens:, :] = got_ref[:, kept:]

    def step(yh, carry):
        for yl in range(2):
            for xh in range(2):
                start = pl.multiple_of((yh * 2 + yl) * 512 + xh * 256, 256)
                columns = pl.ds(start, 256)
                product = lax.dot_general(
                    jnp.concatenate([kept_ref[:, columns], got_ref[:, columns]], axis=0),
                    keys[...],
                    (((0,), (0,)), ((), ())),
                    preferred_element_type=jnp.float32,
                )
                product = product.astype(jnp.bfloat16).reshape(4, 2, 2, 16, 512)
                for zl in range(2):
                    for xl in range(2):
                        out[yl, xl, zl, yh, xh] = product[:, zl, xl]
            store(yh, yl).start()
        return carry

    lax.fori_loop(0, 4, step, 0)
    for yh in range(4):
        for yl in range(2):
            store(yh, yl).wait()


SMEM = pl.BlockSpec(memory_space=pltpu.MemorySpace.SMEM)
HBM = pl.BlockSpec(memory_space=pltpu.MemorySpace.HBM)
VMEM = pl.BlockSpec(memory_space=pltpu.MemorySpace.VMEM)


def own_part(core, own, key):
    tokens, width = own.shape
    sent = (tokens, width // 2 + key.shape[1])
    return pl.pallas_call(
        own_kernel,
        in_specs=[SMEM, HBM, HBM],
        out_specs=[HBM, VMEM, VMEM],
        out_shape=[
            jax.ShapeDtypeStruct(sent, jnp.bfloat16),
            jax.ShapeDtypeStruct((tokens, width // 2), jnp.bfloat16),
            jax.ShapeDtypeStruct(key.shape, jnp.bfloat16),
        ],
        scratch_shapes=[
            pltpu.VMEM(own.shape, jnp.bfloat16),
            pltpu.VMEM(key.shape, jnp.bfloat16),
            pltpu.VMEM(sent, jnp.bfloat16),
            pltpu.SemaphoreType.DMA((PIECES + 1,)),
            pltpu.SemaphoreType.DMA((PIECES + 1,)),
        ],
        compiler_params=pltpu.CompilerParams(vmem_limit_bytes=12 * 1024 * 1024),
        cost_estimate=pl.CostEstimate(
            flops=4 * tokens * width, bytes_accessed=5 * 1024 * 1024, transcendentals=0
        ),
    )(core, own, key)


def pair_partial(kept, scaled, got):
    tokens, width = kept.shape
    proj = scaled.shape[1]
    shape = (2, 2, 2, 4, 2, 4, 16, proj)
    return pl.pallas_call(
        pair_kernel,
        in_specs=[VMEM, VMEM, VMEM],
        out_specs=HBM,
        out_shape=jax.ShapeDtypeStruct(shape, jnp.bfloat16),
        scratch_shapes=[
            pltpu.VMEM((2 * tokens, proj), jnp.bfloat16),
            pltpu.VMEM(shape, jnp.bfloat16),
            pltpu.SemaphoreType.DMA((2, 4)),
        ],
        compiler_params=pltpu.CompilerParams(vmem_limit_bytes=48 * 1024 * 1024),
        cost_estimate=pl.CostEstimate(
            flops=4 * tokens * width * proj, bytes_accessed=9 * 1024 * 1024, transcendentals=0
        ),
    )(kept, scaled, got)


def sum_kernel(value_ref, out_ref, out, out_sems):
    sources, blocks = value_ref.shape[:2]
    part = blocks // PIECES

    def store(piece):
        place = pl.ds(piece * part, part)
        return pltpu.make_async_copy(out.at[place], out_ref.at[place], out_sems.at[piece])

    for piece in range(PIECES):

        def add(i, carry):
            place = piece * part + i
            total = value_ref[0, place].astype(jnp.float32)
            for source in range(1, sources):
                total = total + value_ref[source, place].astype(jnp.float32)
            out[place] = total.astype(jnp.bfloat16)
            return carry

        lax.fori_loop(0, part, add, 0)
        store(piece).start()
    for piece in range(PIECES):
        store(piece).wait()


def near_sum(value):
    return pl.pallas_call(
        sum_kernel,
        in_specs=[VMEM],
        out_specs=HBM,
        out_shape=jax.ShapeDtypeStruct(value.shape[1:], jnp.bfloat16),
        scratch_shapes=[
            pltpu.VMEM(value.shape[1:], jnp.bfloat16),
            pltpu.SemaphoreType.DMA((PIECES,)),
        ],
        compiler_params=pltpu.CompilerParams(vmem_limit_bytes=12 * 1024 * 1024),
        cost_estimate=pl.CostEstimate(
            flops=value.size, bytes_accessed=5 * 1024 * 1024, transcendentals=0
        ),
    )(value)


def exchange(value, axes, groups=None):
    return lax.all_to_all(
        value, axes, split_axis=0, concat_axis=0, axis_index_groups=groups, tiled=True
    )


def summed(value):
    return jnp.sum(value.astype(jnp.float32), axis=0)


def on_device(
    hidden_in,
    key_grad,
    gain_second,
    weight_second,
    weight_main,
    weight_m,
    weight_v,
    gain_main,
    gain_m,
    gain_v,
):
    node = lax.axis_index(NODE)
    rows = lax.dynamic_slice_in_dim(weight_second, node * 16, 16, 0)
    gains = lax.dynamic_slice_in_dim(gain_second, node * 16, 16, 0)
    pairs = [
        (m * 16 + g, (2 * g + m // 16) * 16 + m % 16) for m in range(32) for g in range(16)
    ]
    packed = jnp.concatenate([rows, jnp.broadcast_to(gains[:, None], (16, 128))], axis=1)

    core = lax.axis_index("core").astype(jnp.int32).reshape(1)
    sent, kept, scaled = own_part(core, hidden_in, key_grad)
    got = lax.ppermute(sent, "core", [(0, 1), (1, 0)])
    packed = lax.ppermute(packed, ALL, pairs)
    partial_value = pair_partial(kept, scaled, got)
    near = exchange(partial_value.reshape(8, 32, 16, 512), ALL, near_groups())
    scaled_grad = summed(exchange(near_sum(near), FAR))

    packed = packed.astype(jnp.float32)
    rows, gains = packed[:, :512], packed[:, 512:513]
    weight_grad = scaled_grad * gains
    gain_grad = jnp.sum(scaled_grad * rows, axis=1)
    weight_new, weight_first, weight_square = adam_update(
        weight_main, weight_m, weight_v, weight_grad
    )
    gain_new, gain_first, gain_square = adam_update(gain_main, gain_m, gain_v, gain_grad)
    return (weight_new, weight_first, weight_square, gain_new, gain_first, gain_square)


def solution(mesh):
    fine = Mesh(mesh.devices.reshape(SIZES), ALL)
    placed = (
        P(ALL, None),
        P(ALL, None),
        P(GROUP),
        P(GROUP, None),
        P(ALL, None),
        P(ALL, None),
        P(ALL, None),
        P(ALL),
        P(ALL),
        P(ALL),
    )
    return jax.shard_map(
        on_device,
        mesh=fine,
        in_specs=placed,
        out_specs=(P(ALL, None),) * 3 + (P(ALL),) * 3,
        check_vma=False,
    )
```

```python
import jax
import jax.numpy as jnp
from jax import lax
from jax.experimental import pallas as pl
from jax.experimental.pallas import tpu as pltpu
from jax.sharding import Mesh, PartitionSpec as P

norm_eps = 1e-05
beta_one = 0.9
beta_two = 0.999
adam_eps = 1e-08
learn_rate = 0.0003
weight_decay = 0.1
bias_one = 1.0 - 2.6561398887587544e-05
bias_two = 1.0 - 0.9047921471137096

SIZES = (4, 2, 2, 2, 4, 2, 2)
ALL = ("yh", "yl", "xh", "core", "zh", "zl", "xl")
NODE, GROUP = ALL[:4], ALL[4:]
FAR = ("yh", "xh", "zh")


def near_groups():
    groups = []
    for core in range(2):
        for ky in range(core, 8, 2):
            for kx in range(core, 4, 2):
                for kz in range(core, 8, 2):
                    members = []
                    for yl in range(2):
                        for xl in range(2):
                            for zl in range(2):
                                y = (ky + (yl != core)) % 8
                                x = (kx + (xl != core)) % 4
                                z = (kz + (zl != core)) % 8
                                members.append((((y * 2 + x // 2) * 2 + core) * 8 + z) * 2 + x % 2)
                    groups.append(members)
    return groups


def adam_update(weights, moment_one, moment_two, gradient):
    moment_new = beta_one * moment_one + (1.0 - beta_one) * gradient
    square_new = beta_two * moment_two + (1.0 - beta_two) * gradient * gradient
    direction = moment_new / bias_one / (jnp.sqrt(square_new / bias_two) + adam_eps)
    return (weights - learn_rate * (direction + weight_decay * weights), moment_new, square_new)


PIECES = 4


def own_kernel(
    core_ref,
    own_ref,
    key_ref,
    send_ref,
    kept_ref,
    scaled_ref,
    own,
    key,
    send,
    own_sems,
    send_sems,
):
    tokens, width = own.shape
    kept = width // 2
    part = width // PIECES

    def fetch(piece):
        columns = pl.ds(piece * part, part)
        return pltpu.make_async_copy(
            own_ref.at[:, columns], own.at[:, columns], own_sems.at[piece]
        )

    def store(piece):
        start = piece * (part // 2)
        columns = pl.ds(start, part // 2 if piece < PIECES else send.shape[1] - start)
        return pltpu.make_async_copy(
            send.at[:, columns], send_ref.at[:, columns], send_sems.at[piece]
        )

    fetch_key = pltpu.make_async_copy(key_ref, key, own_sems.at[PIECES])
    for piece in range(PIECES):
        fetch(piece).start()
    fetch_key.start()
    total = jnp.zeros((tokens, 128), jnp.float32)
    for piece in range(PIECES):
        fetch(piece).wait()

        def add(i, total):
            block = own[:, pl.ds(pl.multiple_of(piece * part + i * 512, 512), 512)]
            block = block.astype(jnp.float32)
            block = block * block
            return (
                total
                + (block[:, :128] + block[:, 128:256])
                + (block[:, 256:384] + block[:, 384:])
            )

        total = lax.fori_loop(0, part // 512, add, total)
        for k in range(piece * part // 512, (piece + 1) * part // 512):
            columns = slice(k * 256, k * 256 + 256)
            start = pl.multiple_of(k * 512 + (1 - core_ref[0]) * 256, 256)
            send[:, columns] = own[:, pl.ds(start, 256)]
            start = pl.multiple_of(k * 512 + core_ref[0] * 256, 256)
            kept_ref[:, columns] = own[:, pl.ds(start, 256)]
        store(piece).start()
    mean = jnp.sum(total, axis=1, keepdims=True) * (1.0 / width)
    fetch_key.wait()
    scaled = key[...].astype(jnp.float32) * lax.rsqrt(mean + norm_eps)
    scaled_ref[...] = scaled.astype(jnp.bfloat16)
    send[:, kept:] = scaled_ref[...]
    store(PIECES).start()
    for piece in range(PIECES + 1):
        store(piece).wait()


def pair_kernel(kept_ref, scaled_ref, got_ref, out_ref, keys, out, out_sems):
    tokens, kept = kept_ref.shape

    def store(yh, yl):
        return pltpu.make_async_copy(
            out.at[yl, :, :, yh], out_ref.at[yl, :, :, yh], out_sems.at[yl, yh]
        )

    keys[:tokens, :] = scaled_ref[...]
    keys[tokens:, :] = got_ref[:, kept:]

    def step(yh, carry):
        for yl in range(2):
            for xh in range(2):
                start = pl.multiple_of((yh * 2 + yl) * 512 + xh * 256, 256)
                columns = pl.ds(start, 256)
                product = lax.dot_general(
                    jnp.concatenate([kept_ref[:, columns], got_ref[:, columns]], axis=0),
                    keys[...],
                    (((0,), (0,)), ((), ())),
                    preferred_element_type=jnp.float32,
                )
                product = product.astype(jnp.bfloat16).reshape(4, 2, 2, 16, 512)
                for zl in range(2):
                    for xl in range(2):
                        out[yl, xl, zl, yh, xh] = product[:, zl, xl]
            store(yh, yl).start()
        return carry

    lax.fori_loop(0, 4, step, 0)
    for yh in range(4):
        for yl in range(2):
            store(yh, yl).wait()


SMEM = pl.BlockSpec(memory_space=pltpu.MemorySpace.SMEM)
HBM = pl.BlockSpec(memory_space=pltpu.MemorySpace.HBM)
VMEM = pl.BlockSpec(memory_space=pltpu.MemorySpace.VMEM)


def own_part(core, own, key):
    tokens, width = own.shape
    sent = (tokens, width // 2 + key.shape[1])
    return pl.pallas_call(
        own_kernel,
        in_specs=[SMEM, HBM, HBM],
        out_specs=[HBM, VMEM, VMEM],
        out_shape=[
            jax.ShapeDtypeStruct(sent, jnp.bfloat16),
            jax.ShapeDtypeStruct((tokens, width // 2), jnp.bfloat16),
            jax.ShapeDtypeStruct(key.shape, jnp.bfloat16),
        ],
        scratch_shapes=[
            pltpu.VMEM(own.shape, jnp.bfloat16),
            pltpu.VMEM(key.shape, jnp.bfloat16),
            pltpu.VMEM(sent, jnp.bfloat16),
            pltpu.SemaphoreType.DMA((PIECES + 1,)),
            pltpu.SemaphoreType.DMA((PIECES + 1,)),
        ],
        compiler_params=pltpu.CompilerParams(vmem_limit_bytes=50 * 1024 * 1024),
        cost_estimate=pl.CostEstimate(
            flops=4 * tokens * width, bytes_accessed=5 * 1024 * 1024, transcendentals=0
        ),
    )(core, own, key)


def pair_partial(kept, scaled, got):
    tokens, width = kept.shape
    proj = scaled.shape[1]
    shape = (2, 2, 2, 4, 2, 4, 16, proj)
    return pl.pallas_call(
        pair_kernel,
        in_specs=[VMEM, VMEM, VMEM],
        out_specs=HBM,
        out_shape=jax.ShapeDtypeStruct(shape, jnp.bfloat16),
        scratch_shapes=[
            pltpu.VMEM((2 * tokens, proj), jnp.bfloat16),
            pltpu.VMEM(shape, jnp.bfloat16),
            pltpu.SemaphoreType.DMA((2, 4)),
        ],
        compiler_params=pltpu.CompilerParams(vmem_limit_bytes=52 * 1024 * 1024),
        cost_estimate=pl.CostEstimate(
            flops=4 * tokens * width * proj, bytes_accessed=9 * 1024 * 1024, transcendentals=0
        ),
    )(kept, scaled, got)


def sum_kernel(value_ref, out_ref, out, out_sems):
    sources, blocks = value_ref.shape[:2]
    part = blocks // PIECES

    def store(piece):
        place = pl.ds(piece * part, part)
        return pltpu.make_async_copy(out.at[place], out_ref.at[place], out_sems.at[piece])

    for piece in range(PIECES):

        def add(i, carry):
            place = piece * part + i
            total = value_ref[0, place].astype(jnp.float32)
            for source in range(1, sources):
                total = total + value_ref[source, place].astype(jnp.float32)
            out[place] = total.astype(jnp.bfloat16)
            return carry

        lax.fori_loop(0, part, add, 0)
        store(piece).start()
    for piece in range(PIECES):
        store(piece).wait()


def near_sum(value):
    return pl.pallas_call(
        sum_kernel,
        in_specs=[VMEM],
        out_specs=HBM,
        out_shape=jax.ShapeDtypeStruct(value.shape[1:], jnp.bfloat16),
        scratch_shapes=[
            pltpu.VMEM(value.shape[1:], jnp.bfloat16),
            pltpu.SemaphoreType.DMA((PIECES,)),
        ],
        compiler_params=pltpu.CompilerParams(vmem_limit_bytes=12 * 1024 * 1024),
        cost_estimate=pl.CostEstimate(
            flops=value.size, bytes_accessed=5 * 1024 * 1024, transcendentals=0
        ),
    )(value)


def exchange(value, axes, groups=None):
    return lax.all_to_all(
        value, axes, split_axis=0, concat_axis=0, axis_index_groups=groups, tiled=True
    )


def summed(value):
    return jnp.sum(value.astype(jnp.float32), axis=0)


def on_device(
    hidden_in,
    key_grad,
    gain_second,
    weight_second,
    weight_main,
    weight_m,
    weight_v,
    gain_main,
    gain_m,
    gain_v,
):
    node = lax.axis_index(NODE)
    rows = lax.dynamic_slice_in_dim(weight_second, node * 16, 16, 0)
    gains = lax.dynamic_slice_in_dim(gain_second, node * 16, 16, 0)
    pairs = [
        (m * 16 + g, (2 * g + m // 16) * 16 + m % 16) for m in range(32) for g in range(16)
    ]
    packed = jnp.concatenate([rows, jnp.broadcast_to(gains[:, None], (16, 128))], axis=1)

    core = lax.axis_index("core").astype(jnp.int32).reshape(1)
    sent, kept, scaled = own_part(core, hidden_in, key_grad)
    got = lax.ppermute(sent, "core", [(0, 1), (1, 0)])
    packed = lax.ppermute(packed, ALL, pairs)
    partial_value = pair_partial(kept, scaled, got)
    partial_value, packed = lax.optimization_barrier((partial_value, packed))
    near = exchange(partial_value.reshape(8, 32, 16, 512), ALL, near_groups())
    scaled_grad = summed(exchange(near_sum(near), FAR))

    packed = packed.astype(jnp.float32)
    rows, gains = packed[:, :512], packed[:, 512:513]
    weight_grad = scaled_grad * gains
    gain_grad = jnp.sum(scaled_grad * rows, axis=1)
    weight_new, weight_first, weight_square = adam_update(
        weight_main, weight_m, weight_v, weight_grad
    )
    gain_new, gain_first, gain_square = adam_update(gain_main, gain_m, gain_v, gain_grad)
    return (weight_new, weight_first, weight_square, gain_new, gain_first, gain_square)


def solution(mesh):
    fine = Mesh(mesh.devices.reshape(SIZES), ALL)
    placed = (
        P(ALL, None),
        P(ALL, None),
        P(GROUP),
        P(GROUP, None),
        P(ALL, None),
        P(ALL, None),
        P(ALL, None),
        P(ALL),
        P(ALL),
        P(ALL),
    )
    return jax.shard_map(
        on_device,
        mesh=fine,
        in_specs=placed,
        out_specs=(P(ALL, None),) * 3 + (P(ALL),) * 3,
        check_vma=False,
    )
```

```python
import functools

import jax
import jax.numpy as jnp
from jax import lax
from jax.experimental import pallas as pl
from jax.experimental.pallas import tpu as pltpu
from jax.sharding import Mesh, PartitionSpec as P

norm_eps = 1e-05
beta_one = 0.9
beta_two = 0.999
adam_eps = 1e-08
learn_rate = 0.0003
weight_decay = 0.1
bias_one = 1.0 - 2.6561398887587544e-05
bias_two = 1.0 - 0.9047921471137096

SIZES = (4, 2, 2, 2, 4, 2, 2)
ALL = ("yh", "yl", "xh", "core", "zh", "zl", "xl")
NODE, GROUP = ALL[:4], ALL[4:]
FAR = ("yh", "xh", "zh")


def near_groups():
    groups = []
    for core in range(2):
        for ky in range(core, 8, 2):
            for kx in range(core, 4, 2):
                for kz in range(core, 8, 2):
                    members = []
                    for yl in range(2):
                        for xl in range(2):
                            for zl in range(2):
                                y = (ky + (yl != core)) % 8
                                x = (kx + (xl != core)) % 4
                                z = (kz + (zl != core)) % 8
                                members.append((((y * 2 + x // 2) * 2 + core) * 8 + z) * 2 + x % 2)
                    groups.append(members)
    return groups


def adam_update(weights, moment_one, moment_two, gradient):
    moment_new = beta_one * moment_one + (1.0 - beta_one) * gradient
    square_new = beta_two * moment_two + (1.0 - beta_two) * gradient * gradient
    direction = moment_new / bias_one / (jnp.sqrt(square_new / bias_two) + adam_eps)
    return (weights - learn_rate * (direction + weight_decay * weights), moment_new, square_new)


PIECES = 4


def own_kernel(
    core_ref,
    own_ref,
    key_ref,
    send_ref,
    kept_ref,
    scaled_ref,
    own,
    key,
    send,
    own_sems,
    send_sems,
):
    tokens, width = own.shape
    kept = width // 2
    part = width // PIECES

    def fetch(piece):
        columns = pl.ds(piece * part, part)
        return pltpu.make_async_copy(
            own_ref.at[:, columns], own.at[:, columns], own_sems.at[piece]
        )

    def store(piece):
        start = piece * (part // 2)
        columns = pl.ds(start, part // 2 if piece < PIECES else send.shape[1] - start)
        return pltpu.make_async_copy(
            send.at[:, columns], send_ref.at[:, columns], send_sems.at[piece]
        )

    fetch_key = pltpu.make_async_copy(key_ref, key, own_sems.at[PIECES])
    for piece in range(PIECES):
        fetch(piece).start()
    fetch_key.start()
    total = jnp.zeros((tokens, 128), jnp.float32)
    for piece in range(PIECES):
        fetch(piece).wait()

        def add(i, total):
            block = own[:, pl.ds(pl.multiple_of(piece * part + i * 512, 512), 512)]
            block = block.astype(jnp.float32)
            block = block * block
            return (
                total
                + (block[:, :128] + block[:, 128:256])
                + (block[:, 256:384] + block[:, 384:])
            )

        total = lax.fori_loop(0, part // 512, add, total)
        for k in range(piece * part // 512, (piece + 1) * part // 512):
            columns = slice(k * 256, k * 256 + 256)
            start = pl.multiple_of(k * 512 + (1 - core_ref[0]) * 256, 256)
            send[:, columns] = own[:, pl.ds(start, 256)]
            start = pl.multiple_of(k * 512 + core_ref[0] * 256, 256)
            kept_ref[:, columns] = own[:, pl.ds(start, 256)]
        store(piece).start()
    mean = jnp.sum(total, axis=1, keepdims=True) * (1.0 / width)
    fetch_key.wait()
    scaled = key[...].astype(jnp.float32) * lax.rsqrt(mean + norm_eps)
    scaled_ref[...] = scaled.astype(jnp.bfloat16)
    send[:, kept:] = scaled_ref[...]
    store(PIECES).start()
    for piece in range(PIECES + 1):
        store(piece).wait()


def pair_kernel(other_y, place_ref, kept_ref, scaled_ref, got_ref, *rest):
    out_refs, (keys, out, out_sems) = rest[:4], rest[4:]
    tokens, kept = kept_ref.shape
    yl, xl, zl = place_ref[1], place_ref[2], place_ref[3]
    if other_y:
        yl = 1 - yl

    def store(yh, near):
        source = out.at[lax.rem(xl + near // 2, 2), lax.rem(zl + near % 2, 2), yh]
        return pltpu.make_async_copy(source, out_refs[near].at[yh], out_sems.at[near, yh])

    keys[:tokens, :] = scaled_ref[...]
    keys[tokens:, :] = got_ref[:, kept:]

    def step(yh, carry):
        for xh in range(2):
            start = pl.multiple_of((yh * 2 + yl) * 512 + xh * 256, 256)
            columns = pl.ds(start, 256)
            product = lax.dot_general(
                jnp.concatenate([kept_ref[:, columns], got_ref[:, columns]], axis=0),
                keys[...],
                (((0,), (0,)), ((), ())),
                preferred_element_type=jnp.float32,
            )
            product = product.astype(jnp.bfloat16).reshape(4, 2, 2, 16, 512)
            for z in range(2):
                for x in range(2):
                    out[x, z, yh, xh] = product[:, z, x]
        for near in range(4):
            store(yh, near).start()
        return carry

    lax.fori_loop(0, 4, step, 0)
    for yh in range(4):
        for near in range(4):
            store(yh, near).wait()


SMEM = pl.BlockSpec(memory_space=pltpu.MemorySpace.SMEM)
HBM = pl.BlockSpec(memory_space=pltpu.MemorySpace.HBM)
VMEM = pl.BlockSpec(memory_space=pltpu.MemorySpace.VMEM)


def own_part(core, own, key):
    tokens, width = own.shape
    sent = (tokens, width // 2 + key.shape[1])
    return pl.pallas_call(
        own_kernel,
        in_specs=[SMEM, HBM, HBM],
        out_specs=[HBM, VMEM, VMEM],
        out_shape=[
            jax.ShapeDtypeStruct(sent, jnp.bfloat16),
            jax.ShapeDtypeStruct((tokens, width // 2), jnp.bfloat16),
            jax.ShapeDtypeStruct(key.shape, jnp.bfloat16),
        ],
        scratch_shapes=[
            pltpu.VMEM(own.shape, jnp.bfloat16),
            pltpu.VMEM(key.shape, jnp.bfloat16),
            pltpu.VMEM(sent, jnp.bfloat16),
            pltpu.SemaphoreType.DMA((PIECES + 1,)),
            pltpu.SemaphoreType.DMA((PIECES + 1,)),
        ],
        compiler_params=pltpu.CompilerParams(vmem_limit_bytes=12 * 1024 * 1024),
        cost_estimate=pl.CostEstimate(
            flops=4 * tokens * width, bytes_accessed=5 * 1024 * 1024, transcendentals=0
        ),
    )(core, own, key)


def pair_partial(place, kept, scaled, got, other_y):
    tokens, width = kept.shape
    proj = scaled.shape[1]
    shape = (4, 2, 4, 16, proj)
    return pl.pallas_call(
        functools.partial(pair_kernel, other_y),
        in_specs=[SMEM, VMEM, VMEM, VMEM],
        out_specs=[HBM] * 4,
        out_shape=[jax.ShapeDtypeStruct(shape, jnp.bfloat16)] * 4,
        scratch_shapes=[
            pltpu.VMEM((2 * tokens, proj), jnp.bfloat16),
            pltpu.VMEM((2, 2) + shape, jnp.bfloat16),
            pltpu.SemaphoreType.DMA((4, 4)),
        ],
        compiler_params=pltpu.CompilerParams(vmem_limit_bytes=16 * 1024 * 1024),
        cost_estimate=pl.CostEstimate(
            flops=2 * tokens * width * proj, bytes_accessed=5 * 1024 * 1024, transcendentals=0
        ),
    )(place, kept, scaled, got)


def sum_kernel(*refs):
    value_refs, (out_ref, out, out_sems) = refs[:-3], refs[-3:]
    blocks = out.shape[0]
    part = blocks // PIECES

    def store(piece):
        place = pl.ds(piece * part, part)
        return pltpu.make_async_copy(out.at[place], out_ref.at[place], out_sems.at[piece])

    for piece in range(PIECES):

        def add(i, carry):
            place = piece * part + i
            total = value_refs[0][place].astype(jnp.float32)
            for value_ref in value_refs[1:]:
                total = total + value_ref[place].astype(jnp.float32)
            out[place] = total.astype(jnp.bfloat16)
            return carry

        lax.fori_loop(0, part, add, 0)
        store(piece).start()
    for piece in range(PIECES):
        store(piece).wait()


def near_sum(values):
    value = values[0]
    return pl.pallas_call(
        sum_kernel,
        in_specs=[VMEM] * len(values),
        out_specs=HBM,
        out_shape=jax.ShapeDtypeStruct(value.shape, jnp.bfloat16),
        scratch_shapes=[
            pltpu.VMEM(value.shape, jnp.bfloat16),
            pltpu.SemaphoreType.DMA((PIECES,)),
        ],
        compiler_params=pltpu.CompilerParams(vmem_limit_bytes=12 * 1024 * 1024),
        cost_estimate=pl.CostEstimate(
            flops=8 * value.size, bytes_accessed=5 * 1024 * 1024, transcendentals=0
        ),
    )(*values)


def exchange(value, axes):
    return lax.all_to_all(value, axes, split_axis=0, concat_axis=0, tiled=True)


def near_exchange(value, groups, near):
    pairs = [(g[i], g[i ^ near]) for g in groups for i in range(8)]
    return lax.ppermute(value, ALL, pairs)


def summed(value):
    return jnp.sum(value.astype(jnp.float32), axis=0)


def on_device(
    hidden_in,
    key_grad,
    gain_second,
    weight_second,
    weight_main,
    weight_m,
    weight_v,
    gain_main,
    gain_m,
    gain_v,
):
    node = lax.axis_index(NODE)
    rows = lax.dynamic_slice_in_dim(weight_second, node * 16, 16, 0)
    gains = lax.dynamic_slice_in_dim(gain_second, node * 16, 16, 0)
    pairs = [
        (m * 16 + g, (2 * g + m // 16) * 16 + m % 16) for m in range(32) for g in range(16)
    ]
    packed = jnp.concatenate([rows, jnp.broadcast_to(gains[:, None], (16, 128))], axis=1)

    place = jnp.stack([lax.axis_index(name) for name in ("core", "yl", "xl", "zl")])
    place = place.astype(jnp.int32)
    sent, kept, scaled = own_part(place, hidden_in, key_grad)
    got = lax.ppermute(sent, "core", [(0, 1), (1, 0)])
    packed = lax.ppermute(packed, ALL, pairs)
    far_y = pair_partial(place, kept, scaled, got, True)
    near_y = pair_partial(place, kept, scaled, got, False)
    groups = near_groups()
    blocks = [near_y[0]]
    blocks += [near_exchange(far_y[i], groups, 4 + i) for i in (3, 2, 1, 0)]
    blocks += [near_exchange(near_y[i], groups, i) for i in (3, 2, 1)]
    near = [block.reshape(32, 16, 512) for block in blocks]
    scaled_grad = summed(exchange(near_sum(near), FAR))

    packed = packed.astype(jnp.float32)
    rows, gains = packed[:, :512], packed[:, 512:513]
    weight_grad = scaled_grad * gains
    gain_grad = jnp.sum(scaled_grad * rows, axis=1)
    weight_new, weight_first, weight_square = adam_update(
        weight_main, weight_m, weight_v, weight_grad
    )
    gain_new, gain_first, gain_square = adam_update(gain_main, gain_m, gain_v, gain_grad)
    return (weight_new, weight_first, weight_square, gain_new, gain_first, gain_square)


def solution(mesh):
    fine = Mesh(mesh.devices.reshape(SIZES), ALL)
    placed = (
        P(ALL, None),
        P(ALL, None),
        P(GROUP),
        P(GROUP, None),
        P(ALL, None),
        P(ALL, None),
        P(ALL, None),
        P(ALL),
        P(ALL),
        P(ALL),
    )
    return jax.shard_map(
        on_device,
        mesh=fine,
        in_specs=placed,
        out_specs=(P(ALL, None),) * 3 + (P(ALL),) * 3,
        check_vma=False,
    )
```

```python
import jax
import jax.numpy as jnp
from jax import lax
from jax.experimental import pallas as pl
from jax.experimental.pallas import tpu as pltpu
from jax.sharding import Mesh, PartitionSpec as P

norm_eps = 1e-05
beta_one = 0.9
beta_two = 0.999
adam_eps = 1e-08
learn_rate = 0.0003
weight_decay = 0.1
bias_one = 1.0 - 2.6561398887587544e-05
bias_two = 1.0 - 0.9047921471137096

SIZES = (4, 2, 2, 2, 4, 2, 2)
ALL = ("yh", "yl", "xh", "core", "zh", "zl", "xl")
NODE, GROUP = ALL[:4], ALL[4:]


def side(place):
    return (place + place // 2 + place // 4) % 2


def exchange_groups():
    near, far = {}, {}
    for y in range(8):
        for x in range(4):
            for core in range(2):
                for z in range(8):
                    device = (((y * 2 + x // 2) * 2 + core) * 8 + z) * 2 + x % 2
                    places = ((y - core) % 8, (x - core) % 4, (z - core) % 8)
                    pair = tuple(place // 2 for place in places)
                    sides = tuple(side(place) for place in places)
                    near.setdefault((core,) + pair, []).append((sides, device))
                    far.setdefault((core,) + sides, []).append((pair, device))
    return [
        [[device for _, device in sorted(members)] for members in groups.values()]
        for groups in (near, far)
    ]


def adam_update(weights, moment_one, moment_two, gradient):
    moment_new = beta_one * moment_one + (1.0 - beta_one) * gradient
    square_new = beta_two * moment_two + (1.0 - beta_two) * gradient * gradient
    direction = moment_new / bias_one / (jnp.sqrt(square_new / bias_two) + adam_eps)
    return (weights - learn_rate * (direction + weight_decay * weights), moment_new, square_new)


PIECES = 4


def own_kernel(
    core_ref,
    own_ref,
    key_ref,
    send_ref,
    kept_ref,
    scaled_ref,
    own,
    key,
    send,
    own_sems,
    send_sems,
):
    tokens, width = own.shape
    kept = width // 2
    part = width // PIECES

    def fetch(piece):
        columns = pl.ds(piece * part, part)
        return pltpu.make_async_copy(
            own_ref.at[:, columns], own.at[:, columns], own_sems.at[piece]
        )

    def store(piece):
        start = piece * (part // 2)
        columns = pl.ds(start, part // 2 if piece < PIECES else send.shape[1] - start)
        return pltpu.make_async_copy(
            send.at[:, columns], send_ref.at[:, columns], send_sems.at[piece]
        )

    fetch_key = pltpu.make_async_copy(key_ref, key, own_sems.at[PIECES])
    for piece in range(PIECES):
        fetch(piece).start()
    fetch_key.start()
    total = jnp.zeros((tokens, 128), jnp.float32)
    for piece in range(PIECES):
        fetch(piece).wait()

        def add(i, total):
            block = own[:, pl.ds(pl.multiple_of(piece * part + i * 512, 512), 512)]
            block = block.astype(jnp.float32)
            block = block * block
            return (
                total
                + (block[:, :128] + block[:, 128:256])
                + (block[:, 256:384] + block[:, 384:])
            )

        total = lax.fori_loop(0, part // 512, add, total)
        for k in range(piece * part // 512, (piece + 1) * part // 512):
            columns = slice(k * 256, k * 256 + 256)
            start = pl.multiple_of(k * 512 + (1 - core_ref[0]) * 256, 256)
            send[:, columns] = own[:, pl.ds(start, 256)]
            start = pl.multiple_of(k * 512 + core_ref[0] * 256, 256)
            kept_ref[:, columns] = own[:, pl.ds(start, 256)]
        store(piece).start()
    mean = jnp.sum(total, axis=1, keepdims=True) * (1.0 / width)
    fetch_key.wait()
    scaled = key[...].astype(jnp.float32) * lax.rsqrt(mean + norm_eps)
    scaled_ref[...] = scaled.astype(jnp.bfloat16)
    send[:, kept:] = scaled_ref[...]
    store(PIECES).start()
    for piece in range(PIECES + 1):
        store(piece).wait()


def pair_kernel(core_ref, kept_ref, scaled_ref, got_ref, out_ref, keys, out, out_sems):
    tokens, kept = kept_ref.shape
    core = core_ref[0]

    def store(side_y, pair_y):
        return pltpu.make_async_copy(
            out.at[side_y, :, pair_y], out_ref.at[side_y, :, pair_y], out_sems.at[side_y, pair_y]
        )

    keys[:tokens, :] = scaled_ref[...]
    keys[tokens:, :] = got_ref[:, kept:]
    places_x = [lax.rem(x + 4 - core, 4) for x in range(4)]
    places_z = [lax.rem(z + 8 - core, 8) for z in range(8)]
    sides_x, pairs_x = [side(p) for p in places_x], [p // 2 for p in places_x]
    sides_z, pairs_z = [side(p) for p in places_z], [p // 2 for p in places_z]

    def step(pair_y, carry):
        for member in range(2):
            place_y = pair_y * 2 + member
            side_y = side(place_y)
            row = lax.rem(place_y + core, 8)
            for xh in range(2):
                columns = pl.ds(pl.multiple_of(row * 512 + xh * 256, 256), 256)
                product = lax.dot_general(
                    jnp.concatenate([kept_ref[:, columns], got_ref[:, columns]], axis=0),
                    keys[...],
                    (((0,), (0,)), ((), ())),
                    preferred_element_type=jnp.float32,
                )
                product = product.astype(jnp.bfloat16).reshape(8, 2, 16, 512)
                for z in range(8):
                    for xl in range(2):
                        x = xh * 2 + xl
                        near = sides_x[x] * 2 + sides_z[z]
                        far = pairs_x[x] * 4 + pairs_z[z]
                        out[side_y, near, pair_y, far] = product[z, xl]
            store(side_y, pair_y).start()
        return carry

    lax.fori_loop(0, 4, step, 0)
    for pair_y in range(4):
        for side_y in range(2):
            store(side_y, pair_y).wait()


SMEM = pl.BlockSpec(memory_space=pltpu.MemorySpace.SMEM)
HBM = pl.BlockSpec(memory_space=pltpu.MemorySpace.HBM)
VMEM = pl.BlockSpec(memory_space=pltpu.MemorySpace.VMEM)


def own_part(core, own, key):
    tokens, width = own.shape
    sent = (tokens, width // 2 + key.shape[1])
    return pl.pallas_call(
        own_kernel,
        in_specs=[SMEM, HBM, HBM],
        out_specs=[HBM, VMEM, VMEM],
        out_shape=[
            jax.ShapeDtypeStruct(sent, jnp.bfloat16),
            jax.ShapeDtypeStruct((tokens, width // 2), jnp.bfloat16),
            jax.ShapeDtypeStruct(key.shape, jnp.bfloat16),
        ],
        scratch_shapes=[
            pltpu.VMEM(own.shape, jnp.bfloat16),
            pltpu.VMEM(key.shape, jnp.bfloat16),
            pltpu.VMEM(sent, jnp.bfloat16),
            pltpu.SemaphoreType.DMA((PIECES + 1,)),
            pltpu.SemaphoreType.DMA((PIECES + 1,)),
        ],
        compiler_params=pltpu.CompilerParams(vmem_limit_bytes=12 * 1024 * 1024),
        cost_estimate=pl.CostEstimate(
            flops=4 * tokens * width, bytes_accessed=5 * 1024 * 1024, transcendentals=0
        ),
    )(core, own, key)


def pair_partial(core, kept, scaled, got):
    tokens, width = kept.shape
    proj = scaled.shape[1]
    shape = (2, 4, 4, 8, 16, proj)
    return pl.pallas_call(
        pair_kernel,
        in_specs=[SMEM, VMEM, VMEM, VMEM],
        out_specs=HBM,
        out_shape=jax.ShapeDtypeStruct(shape, jnp.bfloat16),
        scratch_shapes=[
            pltpu.VMEM((2 * tokens, proj), jnp.bfloat16),
            pltpu.VMEM(shape, jnp.bfloat16),
            pltpu.SemaphoreType.DMA((2, 4)),
        ],
        compiler_params=pltpu.CompilerParams(vmem_limit_bytes=48 * 1024 * 1024),
        cost_estimate=pl.CostEstimate(
            flops=4 * tokens * width * proj, bytes_accessed=9 * 1024 * 1024, transcendentals=0
        ),
    )(core, kept, scaled, got)


def sum_kernel(value_ref, out_ref, out, out_sems):
    sources, blocks = value_ref.shape[:2]
    part = blocks // PIECES

    def store(piece):
        place = pl.ds(piece * part, part)
        return pltpu.make_async_copy(out.at[place], out_ref.at[place], out_sems.at[piece])

    for piece in range(PIECES):

        def add(i, carry):
            place = piece * part + i
            total = value_ref[0, place].astype(jnp.float32)
            for source in range(1, sources):
                total = total + value_ref[source, place].astype(jnp.float32)
            out[place] = total.astype(jnp.bfloat16)
            return carry

        lax.fori_loop(0, part, add, 0)
        store(piece).start()
    for piece in range(PIECES):
        store(piece).wait()


def near_sum(value):
    return pl.pallas_call(
        sum_kernel,
        in_specs=[VMEM],
        out_specs=HBM,
        out_shape=jax.ShapeDtypeStruct(value.shape[1:], jnp.bfloat16),
        scratch_shapes=[
            pltpu.VMEM(value.shape[1:], jnp.bfloat16),
            pltpu.SemaphoreType.DMA((PIECES,)),
        ],
        compiler_params=pltpu.CompilerParams(vmem_limit_bytes=12 * 1024 * 1024),
        cost_estimate=pl.CostEstimate(
            flops=value.size, bytes_accessed=5 * 1024 * 1024, transcendentals=0
        ),
    )(value)


def exchange(value, groups):
    return lax.all_to_all(
        value, ALL, split_axis=0, concat_axis=0, axis_index_groups=groups, tiled=True
    )


def summed(value):
    return jnp.sum(value.astype(jnp.float32), axis=0)


def on_device(
    hidden_in,
    key_grad,
    gain_second,
    weight_second,
    weight_main,
    weight_m,
    weight_v,
    gain_main,
    gain_m,
    gain_v,
):
    node = lax.axis_index(NODE)
    rows = lax.dynamic_slice_in_dim(weight_second, node * 16, 16, 0)
    gains = lax.dynamic_slice_in_dim(gain_second, node * 16, 16, 0)
    pairs = [
        (m * 16 + g, (2 * g + m // 16) * 16 + m % 16) for m in range(32) for g in range(16)
    ]
    packed = jnp.concatenate([rows, jnp.broadcast_to(gains[:, None], (16, 128))], axis=1)

    core = lax.axis_index("core").astype(jnp.int32).reshape(1)
    sent, kept, scaled = own_part(core, hidden_in, key_grad)
    got = lax.ppermute(sent, "core", [(0, 1), (1, 0)])
    packed = lax.ppermute(packed, ALL, pairs)
    partial_value = pair_partial(core, kept, scaled, got)
    near_groups, far_groups = exchange_groups()
    near = exchange(partial_value.reshape(8, 32, 16, 512), near_groups)
    scaled_grad = summed(exchange(near_sum(near), far_groups))

    packed = packed.astype(jnp.float32)
    rows, gains = packed[:, :512], packed[:, 512:513]
    weight_grad = scaled_grad * gains
    gain_grad = jnp.sum(scaled_grad * rows, axis=1)
    weight_new, weight_first, weight_square = adam_update(
        weight_main, weight_m, weight_v, weight_grad
    )
    gain_new, gain_first, gain_square = adam_update(gain_main, gain_m, gain_v, gain_grad)
    return (weight_new, weight_first, weight_square, gain_new, gain_first, gain_square)


def solution(mesh):
    fine = Mesh(mesh.devices.reshape(SIZES), ALL)
    placed = (
        P(ALL, None),
        P(ALL, None),
        P(GROUP),
        P(GROUP, None),
        P(ALL, None),
        P(ALL, None),
        P(ALL, None),
        P(ALL),
        P(ALL),
        P(ALL),
    )
    return jax.shard_map(
        on_device,
        mesh=fine,
        in_specs=placed,
        out_specs=(P(ALL, None),) * 3 + (P(ALL),) * 3,
        check_vma=False,
    )
```

```python
import jax
import jax.numpy as jnp
from jax import lax
from jax.experimental import pallas as pl
from jax.experimental.pallas import tpu as pltpu
from jax.sharding import Mesh, PartitionSpec as P

norm_eps = 1e-05
beta_one = 0.9
beta_two = 0.999
adam_eps = 1e-08
learn_rate = 0.0003
weight_decay = 0.1
bias_one = 1.0 - 2.6561398887587544e-05
bias_two = 1.0 - 0.9047921471137096

SIZES = (4, 2, 2, 2, 4, 2, 2)
ALL = ("yh", "yl", "xh", "core", "zh", "zl", "xl")
GROUP = ALL[4:]


def side(place):
    return (place + place // 2 + place // 4) % 2


def exchange_groups():
    near, far = {}, {}
    for y in range(8):
        for x in range(4):
            for core in range(2):
                for z in range(8):
                    device = (((y * 2 + x // 2) * 2 + core) * 8 + z) * 2 + x % 2
                    places = ((y - core) % 8, (x - core) % 4, (z - core) % 8)
                    pair = tuple(place // 2 for place in places)
                    sides = tuple(side(place) for place in places)
                    near.setdefault((core,) + pair, []).append((sides, device))
                    far.setdefault((core,) + sides, []).append((pair, device))
    return [
        [[device for _, device in sorted(members)] for members in groups.values()]
        for groups in (near, far)
    ]


def adam_update(weights, moment_one, moment_two, gradient):
    moment_new = beta_one * moment_one + (1.0 - beta_one) * gradient
    square_new = beta_two * moment_two + (1.0 - beta_two) * gradient * gradient
    direction = moment_new / bias_one / (jnp.sqrt(square_new / bias_two) + adam_eps)
    return (weights - learn_rate * (direction + weight_decay * weights), moment_new, square_new)


PIECES = 4


def own_kernel(
    core_ref,
    own_ref,
    key_ref,
    send_ref,
    kept_ref,
    scaled_ref,
    own,
    key,
    send,
    own_sems,
    send_sems,
):
    tokens, width = own.shape
    kept = width // 2
    part = width // PIECES

    def fetch(piece):
        columns = pl.ds(piece * part, part)
        return pltpu.make_async_copy(
            own_ref.at[:, columns], own.at[:, columns], own_sems.at[piece]
        )

    def store(piece):
        start = piece * (part // 2)
        columns = pl.ds(start, part // 2 if piece < PIECES else send.shape[1] - start)
        return pltpu.make_async_copy(
            send.at[:, columns], send_ref.at[:, columns], send_sems.at[piece]
        )

    fetch_key = pltpu.make_async_copy(key_ref, key, own_sems.at[PIECES])
    for piece in range(PIECES):
        fetch(piece).start()
    fetch_key.start()
    total = jnp.zeros((tokens, 128), jnp.float32)
    for piece in range(PIECES):
        fetch(piece).wait()

        def add(i, total):
            block = own[:, pl.ds(pl.multiple_of(piece * part + i * 512, 512), 512)]
            block = block.astype(jnp.float32)
            block = block * block
            return (
                total
                + (block[:, :128] + block[:, 128:256])
                + (block[:, 256:384] + block[:, 384:])
            )

        total = lax.fori_loop(0, part // 512, add, total)
        for k in range(piece * part // 512, (piece + 1) * part // 512):
            columns = slice(k * 256, k * 256 + 256)
            start = pl.multiple_of(k * 512 + (1 - core_ref[0]) * 256, 256)
            send[:, columns] = own[:, pl.ds(start, 256)]
            start = pl.multiple_of(k * 512 + core_ref[0] * 256, 256)
            kept_ref[:, columns] = own[:, pl.ds(start, 256)]
        store(piece).start()
    mean = jnp.sum(total, axis=1, keepdims=True) * (1.0 / width)
    fetch_key.wait()
    scaled = key[...].astype(jnp.float32) * lax.rsqrt(mean + norm_eps)
    scaled_ref[...] = scaled.astype(jnp.bfloat16)
    send[:, kept:] = scaled_ref[...]
    store(PIECES).start()
    for piece in range(PIECES + 1):
        store(piece).wait()


def pair_kernel(core_ref, kept_ref, scaled_ref, got_ref, out_ref, keys, out, out_sems):
    tokens, kept = kept_ref.shape
    core = core_ref[0]

    def store(side_y, pair_y):
        return pltpu.make_async_copy(
            out.at[side_y, :, pair_y], out_ref.at[side_y, :, pair_y], out_sems.at[side_y, pair_y]
        )

    keys[:tokens, :] = scaled_ref[...]
    keys[tokens:, :] = got_ref[:, kept:]
    places_x = [lax.rem(x + 4 - core, 4) for x in range(4)]
    places_z = [lax.rem(z + 8 - core, 8) for z in range(8)]
    sides_x, pairs_x = [side(p) for p in places_x], [p // 2 for p in places_x]
    sides_z, pairs_z = [side(p) for p in places_z], [p // 2 for p in places_z]

    def step(pair_y, carry):
        for member in range(2):
            place_y = pair_y * 2 + member
            side_y = side(place_y)
            row = lax.rem(place_y + core, 8)
            for xh in range(2):
                columns = pl.ds(pl.multiple_of(row * 512 + xh * 256, 256), 256)
                product = lax.dot_general(
                    jnp.concatenate([kept_ref[:, columns], got_ref[:, columns]], axis=0),
                    keys[...],
                    (((0,), (0,)), ((), ())),
                    preferred_element_type=jnp.float32,
                )
                product = product.astype(jnp.bfloat16).reshape(8, 2, 16, 512)
                for z in range(8):
                    for xl in range(2):
                        x = xh * 2 + xl
                        near = sides_x[x] * 2 + sides_z[z]
                        far = pairs_x[x] * 4 + pairs_z[z]
                        out[side_y, near, pair_y, far] = product[z, xl]
            store(side_y, pair_y).start()
        return carry

    lax.fori_loop(0, 4, step, 0)
    for pair_y in range(4):
        for side_y in range(2):
            store(side_y, pair_y).wait()


SMEM = pl.BlockSpec(memory_space=pltpu.MemorySpace.SMEM)
HBM = pl.BlockSpec(memory_space=pltpu.MemorySpace.HBM)
VMEM = pl.BlockSpec(memory_space=pltpu.MemorySpace.VMEM)


def own_part(core, own, key):
    tokens, width = own.shape
    sent = (tokens, width // 2 + key.shape[1])
    return pl.pallas_call(
        own_kernel,
        in_specs=[SMEM, HBM, HBM],
        out_specs=[HBM, VMEM, VMEM],
        out_shape=[
            jax.ShapeDtypeStruct(sent, jnp.bfloat16),
            jax.ShapeDtypeStruct((tokens, width // 2), jnp.bfloat16),
            jax.ShapeDtypeStruct(key.shape, jnp.bfloat16),
        ],
        scratch_shapes=[
            pltpu.VMEM(own.shape, jnp.bfloat16),
            pltpu.VMEM(key.shape, jnp.bfloat16),
            pltpu.VMEM(sent, jnp.bfloat16),
            pltpu.SemaphoreType.DMA((PIECES + 1,)),
            pltpu.SemaphoreType.DMA((PIECES + 1,)),
        ],
        compiler_params=pltpu.CompilerParams(vmem_limit_bytes=50 * 1024 * 1024),
        cost_estimate=pl.CostEstimate(
            flops=4 * tokens * width, bytes_accessed=5 * 1024 * 1024, transcendentals=0
        ),
    )(core, own, key)


def pair_partial(core, kept, scaled, got):
    tokens, width = kept.shape
    proj = scaled.shape[1]
    shape = (2, 4, 4, 8, 16, proj)
    return pl.pallas_call(
        pair_kernel,
        in_specs=[SMEM, VMEM, VMEM, VMEM],
        out_specs=HBM,
        out_shape=jax.ShapeDtypeStruct(shape, jnp.bfloat16),
        scratch_shapes=[
            pltpu.VMEM((2 * tokens, proj), jnp.bfloat16),
            pltpu.VMEM(shape, jnp.bfloat16),
            pltpu.SemaphoreType.DMA((2, 4)),
        ],
        compiler_params=pltpu.CompilerParams(vmem_limit_bytes=48 * 1024 * 1024),
        cost_estimate=pl.CostEstimate(
            flops=4 * tokens * width * proj, bytes_accessed=9 * 1024 * 1024, transcendentals=0
        ),
    )(core, kept, scaled, got)


def sum_kernel(value_ref, out_ref, out, out_sems):
    sources, blocks = value_ref.shape[:2]
    part = blocks // PIECES

    def store(piece):
        place = pl.ds(piece * part, part)
        return pltpu.make_async_copy(out.at[place], out_ref.at[place], out_sems.at[piece])

    for piece in range(PIECES):

        def add(i, carry):
            place = piece * part + i
            total = value_ref[0, place].astype(jnp.float32)
            for source in range(1, sources):
                total = total + value_ref[source, place].astype(jnp.float32)
            out[place] = total.astype(jnp.bfloat16)
            return carry

        lax.fori_loop(0, part, add, 0)
        store(piece).start()
    for piece in range(PIECES):
        store(piece).wait()


def near_sum(value):
    return pl.pallas_call(
        sum_kernel,
        in_specs=[VMEM],
        out_specs=HBM,
        out_shape=jax.ShapeDtypeStruct(value.shape[1:], jnp.bfloat16),
        scratch_shapes=[
            pltpu.VMEM(value.shape[1:], jnp.bfloat16),
            pltpu.SemaphoreType.DMA((PIECES,)),
        ],
        compiler_params=pltpu.CompilerParams(vmem_limit_bytes=12 * 1024 * 1024),
        cost_estimate=pl.CostEstimate(
            flops=value.size, bytes_accessed=5 * 1024 * 1024, transcendentals=0
        ),
    )(value)


def exchange(value, groups):
    return lax.all_to_all(
        value, ALL, split_axis=0, concat_axis=0, axis_index_groups=groups, tiled=True
    )


def summed(value):
    return jnp.sum(value.astype(jnp.float32), axis=0)


def on_device(
    hidden_in,
    key_grad,
    gain_second,
    weight_second,
    weight_main,
    weight_m,
    weight_v,
    gain_main,
    gain_m,
    gain_v,
):
    y = lax.axis_index(("yh", "yl"))
    target = (lax.axis_index("core") * 8 + lax.rem(y + 4, 8)) * 2 + lax.axis_index("xh")
    rows = lax.dynamic_slice_in_dim(weight_second, target * 16, 16, 0)
    gains = lax.dynamic_slice_in_dim(gain_second, target * 16, 16, 0)
    number = lambda y, xh, core, z, xl: (((y * 2 + xh) * 2 + core) * 8 + z) * 2 + xl
    pairs = [
        (number((z + 4) % 8, xl, core, y, xh), number(y, xh, core, z, xl))
        for y in range(8)
        for xh in range(2)
        for core in range(2)
        for z in range(8)
        for xl in range(2)
    ]
    packed = jnp.concatenate([rows, jnp.broadcast_to(gains[:, None], (16, 128))], axis=1)

    core = lax.axis_index("core").astype(jnp.int32).reshape(1)
    sent, kept, scaled = own_part(core, hidden_in, key_grad)
    got = lax.ppermute(sent, "core", [(0, 1), (1, 0)])
    packed = lax.ppermute(packed, ALL, pairs)
    partial_value = pair_partial(core, kept, scaled, got)
    near_groups, far_groups = exchange_groups()
    near = exchange(partial_value.reshape(8, 32, 16, 512), near_groups)
    scaled_grad = summed(exchange(near_sum(near), far_groups))

    packed = packed.astype(jnp.float32)
    rows, gains = packed[:, :512], packed[:, 512:513]
    weight_grad = scaled_grad * gains
    gain_grad = jnp.sum(scaled_grad * rows, axis=1)
    weight_new, weight_first, weight_square = adam_update(
        weight_main, weight_m, weight_v, weight_grad
    )
    gain_new, gain_first, gain_square = adam_update(gain_main, gain_m, gain_v, gain_grad)
    return (weight_new, weight_first, weight_square, gain_new, gain_first, gain_square)


def solution(mesh):
    fine = Mesh(mesh.devices.reshape(SIZES), ALL)
    placed = (
        P(ALL, None),
        P(ALL, None),
        P(GROUP),
        P(GROUP, None),
        P(ALL, None),
        P(ALL, None),
        P(ALL, None),
        P(ALL),
        P(ALL),
        P(ALL),
    )
    return jax.shard_map(
        on_device,
        mesh=fine,
        in_specs=placed,
        out_specs=(P(ALL, None),) * 3 + (P(ALL),) * 3,
        check_vma=False,
    )
```

```python
import jax
import jax.numpy as jnp
from jax import lax
from jax.experimental import pallas as pl
from jax.experimental.pallas import tpu as pltpu
from jax.sharding import Mesh, PartitionSpec as P

norm_eps = 1e-05
beta_one = 0.9
beta_two = 0.999
adam_eps = 1e-08
learn_rate = 0.0003
weight_decay = 0.1
bias_one = 1.0 - 2.6561398887587544e-05
bias_two = 1.0 - 0.9047921471137096

SIZES = (4, 2, 2, 2, 4, 2, 2)
ALL = ("yh", "yl", "xh", "core", "zh", "zl", "xl")
GROUP = ALL[4:]


def side(place):
    return (place + place // 2 + place // 4) % 2


def exchange_groups():
    near, far = {}, {}
    for y in range(8):
        for x in range(4):
            for core in range(2):
                for z in range(8):
                    device = (((y * 2 + x // 2) * 2 + core) * 8 + z) * 2 + x % 2
                    places = ((y - core) % 8, (x - core) % 4, (z - core) % 8)
                    pair = tuple(place // 2 for place in places)
                    sides = tuple(side(place) for place in places)
                    near.setdefault((core,) + pair, []).append((sides, device))
                    far.setdefault((core,) + sides, []).append((pair, device))
    return [
        [[device for _, device in sorted(members)] for members in groups.values()]
        for groups in (near, far)
    ]


def adam_update(weights, moment_one, moment_two, gradient):
    moment_new = beta_one * moment_one + (1.0 - beta_one) * gradient
    square_new = beta_two * moment_two + (1.0 - beta_two) * gradient * gradient
    direction = moment_new / bias_one / (jnp.sqrt(square_new / bias_two) + adam_eps)
    return (weights - learn_rate * (direction + weight_decay * weights), moment_new, square_new)


PIECES = 4


def own_kernel(
    core_ref,
    own_ref,
    key_ref,
    send_ref,
    kept_ref,
    scaled_ref,
    own,
    key,
    send,
    own_sems,
    send_sems,
):
    tokens, width = own.shape
    kept = width // 2
    part = width // PIECES

    def fetch(piece):
        columns = pl.ds(piece * part, part)
        return pltpu.make_async_copy(
            own_ref.at[:, columns], own.at[:, columns], own_sems.at[piece]
        )

    def store(piece):
        start = piece * (part // 2)
        columns = pl.ds(start, part // 2 if piece < PIECES else send.shape[1] - start)
        return pltpu.make_async_copy(
            send.at[:, columns], send_ref.at[:, columns], send_sems.at[piece]
        )

    fetch_key = pltpu.make_async_copy(key_ref, key, own_sems.at[PIECES])
    for piece in range(PIECES):
        fetch(piece).start()
    fetch_key.start()
    total = jnp.zeros((tokens, 128), jnp.float32)
    for piece in range(PIECES):
        fetch(piece).wait()

        def add(i, total):
            block = own[:, pl.ds(pl.multiple_of(piece * part + i * 512, 512), 512)]
            block = block.astype(jnp.float32)
            block = block * block
            return (
                total
                + (block[:, :128] + block[:, 128:256])
                + (block[:, 256:384] + block[:, 384:])
            )

        total = lax.fori_loop(0, part // 512, add, total)
        for k in range(piece * part // 512, (piece + 1) * part // 512):
            columns = slice(k * 256, k * 256 + 256)
            start = pl.multiple_of(k * 512 + (1 - core_ref[0]) * 256, 256)
            send[:, columns] = own[:, pl.ds(start, 256)]
            start = pl.multiple_of(k * 512 + core_ref[0] * 256, 256)
            kept_ref[:, columns] = own[:, pl.ds(start, 256)]
        store(piece).start()
    mean = jnp.sum(total, axis=1, keepdims=True) * (1.0 / width)
    fetch_key.wait()
    scaled = key[...].astype(jnp.float32) * lax.rsqrt(mean + norm_eps)
    scaled_ref[...] = scaled.astype(jnp.bfloat16)
    send[:, kept:] = scaled_ref[...]
    store(PIECES).start()
    for piece in range(PIECES + 1):
        store(piece).wait()


def pair_kernel(core_ref, kept_ref, scaled_ref, got_ref, out_ref, keys, out, out_sems):
    tokens, kept = kept_ref.shape
    core = core_ref[0]

    def store(side_y, pair_y):
        return pltpu.make_async_copy(
            out.at[side_y, :, pair_y], out_ref.at[side_y, :, pair_y], out_sems.at[side_y, pair_y]
        )

    keys[:tokens, :] = scaled_ref[...]
    keys[tokens:, :] = got_ref[:, kept:]
    places_x = [lax.rem(x + 4 - core, 4) for x in range(4)]
    places_z = [lax.rem(z + 8 - core, 8) for z in range(8)]
    sides_x, pairs_x = [side(p) for p in places_x], [p // 2 for p in places_x]
    sides_z, pairs_z = [side(p) for p in places_z], [p // 2 for p in places_z]

    def step(pair_y, carry):
        for member in range(2):
            place_y = pair_y * 2 + member
            side_y = side(place_y)
            row = lax.rem(place_y + core, 8)
            for xh in range(2):
                columns = pl.ds(pl.multiple_of(row * 512 + xh * 256, 256), 256)
                product = lax.dot_general(
                    jnp.concatenate([kept_ref[:, columns], got_ref[:, columns]], axis=0),
                    keys[...],
                    (((0,), (0,)), ((), ())),
                    preferred_element_type=jnp.float32,
                )
                product = product.astype(jnp.bfloat16).reshape(8, 2, 16, 512)
                for z in range(8):
                    for xl in range(2):
                        x = xh * 2 + xl
                        near = sides_x[x] * 2 + sides_z[z]
                        far = pairs_x[x] * 4 + pairs_z[z]
                        out[side_y, near, pair_y, far] = product[z, xl]
            store(side_y, pair_y).start()
        return carry

    lax.fori_loop(0, 4, step, 0)
    for pair_y in range(4):
        for side_y in range(2):
            store(side_y, pair_y).wait()


SMEM = pl.BlockSpec(memory_space=pltpu.MemorySpace.SMEM)
HBM = pl.BlockSpec(memory_space=pltpu.MemorySpace.HBM)
VMEM = pl.BlockSpec(memory_space=pltpu.MemorySpace.VMEM)


def own_part(core, own, key):
    tokens, width = own.shape
    sent = (tokens, width // 2 + key.shape[1])
    return pl.pallas_call(
        own_kernel,
        in_specs=[SMEM, HBM, HBM],
        out_specs=[HBM, VMEM, VMEM],
        out_shape=[
            jax.ShapeDtypeStruct(sent, jnp.bfloat16),
            jax.ShapeDtypeStruct((tokens, width // 2), jnp.bfloat16),
            jax.ShapeDtypeStruct(key.shape, jnp.bfloat16),
        ],
        scratch_shapes=[
            pltpu.VMEM(own.shape, jnp.bfloat16),
            pltpu.VMEM(key.shape, jnp.bfloat16),
            pltpu.VMEM(sent, jnp.bfloat16),
            pltpu.SemaphoreType.DMA((PIECES + 1,)),
            pltpu.SemaphoreType.DMA((PIECES + 1,)),
        ],
        compiler_params=pltpu.CompilerParams(vmem_limit_bytes=50 * 1024 * 1024),
        cost_estimate=pl.CostEstimate(
            flops=4 * tokens * width, bytes_accessed=5 * 1024 * 1024, transcendentals=0
        ),
    )(core, own, key)


def pair_partial(core, kept, scaled, got):
    tokens, width = kept.shape
    proj = scaled.shape[1]
    shape = (2, 4, 4, 8, 16, proj)
    return pl.pallas_call(
        pair_kernel,
        in_specs=[SMEM, VMEM, VMEM, VMEM],
        out_specs=HBM,
        out_shape=jax.ShapeDtypeStruct(shape, jnp.bfloat16),
        scratch_shapes=[
            pltpu.VMEM((2 * tokens, proj), jnp.bfloat16),
            pltpu.VMEM(shape, jnp.bfloat16),
            pltpu.SemaphoreType.DMA((2, 4)),
        ],
        compiler_params=pltpu.CompilerParams(vmem_limit_bytes=48 * 1024 * 1024),
        cost_estimate=pl.CostEstimate(
            flops=4 * tokens * width * proj, bytes_accessed=9 * 1024 * 1024, transcendentals=0
        ),
    )(core, kept, scaled, got)


def sum_kernel(value_ref, out_ref, out, out_sems):
    sources, blocks = value_ref.shape[:2]
    part = blocks // PIECES

    def store(piece):
        place = pl.ds(piece * part, part)
        return pltpu.make_async_copy(out.at[place], out_ref.at[place], out_sems.at[piece])

    for piece in range(PIECES):

        def add(i, carry):
            place = piece * part + i
            total = value_ref[0, place].astype(jnp.float32)
            for source in range(1, sources):
                total = total + value_ref[source, place].astype(jnp.float32)
            out[place] = total.astype(jnp.bfloat16)
            return carry

        lax.fori_loop(0, part, add, 0)
        store(piece).start()
    for piece in range(PIECES):
        store(piece).wait()


def near_sum(value):
    return pl.pallas_call(
        sum_kernel,
        in_specs=[VMEM],
        out_specs=HBM,
        out_shape=jax.ShapeDtypeStruct(value.shape[1:], jnp.bfloat16),
        scratch_shapes=[
            pltpu.VMEM(value.shape[1:], jnp.bfloat16),
            pltpu.SemaphoreType.DMA((PIECES,)),
        ],
        compiler_params=pltpu.CompilerParams(vmem_limit_bytes=12 * 1024 * 1024),
        cost_estimate=pl.CostEstimate(
            flops=value.size, bytes_accessed=5 * 1024 * 1024, transcendentals=0
        ),
    )(value)


def exchange(value, groups):
    return lax.all_to_all(
        value, ALL, split_axis=0, concat_axis=0, axis_index_groups=groups, tiled=True
    )


def summed(value):
    return jnp.sum(value.astype(jnp.float32), axis=0)


def on_device(
    hidden_in,
    key_grad,
    gain_second,
    weight_second,
    weight_main,
    weight_m,
    weight_v,
    gain_main,
    gain_m,
    gain_v,
):
    y = lax.axis_index(("yh", "yl"))
    target = (lax.axis_index("core") * 8 + lax.rem(y + 4, 8)) * 2 + lax.axis_index("xh")
    rows = lax.dynamic_slice_in_dim(weight_second, target * 16, 16, 0)
    gains = lax.dynamic_slice_in_dim(gain_second, target * 16, 16, 0)
    number = lambda y, xh, core, z, xl: (((y * 2 + xh) * 2 + core) * 8 + z) * 2 + xl
    pairs = [
        (number((z + 4) % 8, xl, core, y, xh), number(y, xh, core, z, xl))
        for y in range(8)
        for xh in range(2)
        for core in range(2)
        for z in range(8)
        for xl in range(2)
    ]
    packed = jnp.concatenate([rows, jnp.broadcast_to(gains[:, None], (16, 128))], axis=1)

    core = lax.axis_index("core").astype(jnp.int32).reshape(1)
    core, packed = lax.optimization_barrier((core, packed))
    sent, kept, scaled = own_part(core, hidden_in, key_grad)
    got = lax.ppermute(sent, "core", [(0, 1), (1, 0)])
    packed = lax.ppermute(packed, ALL, pairs)
    partial_value = pair_partial(core, kept, scaled, got)
    near_groups, far_groups = exchange_groups()
    near = exchange(partial_value.reshape(8, 32, 16, 512), near_groups)
    scaled_grad = summed(exchange(near_sum(near), far_groups))

    packed = packed.astype(jnp.float32)
    rows, gains = packed[:, :512], packed[:, 512:513]
    weight_grad = scaled_grad * gains
    gain_grad = jnp.sum(scaled_grad * rows, axis=1)
    weight_new, weight_first, weight_square = adam_update(
        weight_main, weight_m, weight_v, weight_grad
    )
    gain_new, gain_first, gain_square = adam_update(gain_main, gain_m, gain_v, gain_grad)
    return (weight_new, weight_first, weight_square, gain_new, gain_first, gain_square)


def solution(mesh):
    fine = Mesh(mesh.devices.reshape(SIZES), ALL)
    placed = (
        P(ALL, None),
        P(ALL, None),
        P(GROUP),
        P(GROUP, None),
        P(ALL, None),
        P(ALL, None),
        P(ALL, None),
        P(ALL),
        P(ALL),
        P(ALL),
    )
    return jax.shard_map(
        on_device,
        mesh=fine,
        in_specs=placed,
        out_specs=(P(ALL, None),) * 3 + (P(ALL),) * 3,
        check_vma=False,
    )
```

```python
import jax
import jax.numpy as jnp
from jax import lax
from jax.experimental import pallas as pl
from jax.experimental.pallas import tpu as pltpu
from jax.sharding import Mesh, PartitionSpec as P

norm_eps = 1e-05
beta_one = 0.9
beta_two = 0.999
adam_eps = 1e-08
learn_rate = 0.0003
weight_decay = 0.1
bias_one = 1.0 - 2.6561398887587544e-05
bias_two = 1.0 - 0.9047921471137096

SIZES = (4, 2, 2, 2, 4, 2, 2)
ALL = ("yh", "yl", "xh", "core", "zh", "zl", "xl")
GROUP = ALL[4:]


def side(place):
    return (place + place // 2 + place // 4) % 2


def exchange_groups():
    near, far = {}, {}
    for y in range(8):
        for x in range(4):
            for core in range(2):
                for z in range(8):
                    device = (((y * 2 + x // 2) * 2 + core) * 8 + z) * 2 + x % 2
                    places = ((y - core) % 8, (x - core) % 4, (z - core) % 8)
                    pair = tuple(place // 2 for place in places)
                    sides = tuple(side(place) for place in places)
                    near.setdefault((core,) + pair, []).append((sides, device))
                    far.setdefault((core,) + sides, []).append((pair, device))
    return [
        [[device for _, device in sorted(members)] for members in groups.values()]
        for groups in (near, far)
    ]


def adam_update(weights, moment_one, moment_two, gradient):
    moment_new = beta_one * moment_one + (1.0 - beta_one) * gradient
    square_new = beta_two * moment_two + (1.0 - beta_two) * gradient * gradient
    direction = moment_new / bias_one / (jnp.sqrt(square_new / bias_two) + adam_eps)
    return (weights - learn_rate * (direction + weight_decay * weights), moment_new, square_new)


PIECES = 8


def own_kernel(
    core_ref,
    own_ref,
    key_ref,
    send_ref,
    kept_ref,
    scaled_ref,
    own,
    key,
    send,
    own_sems,
    send_sems,
):
    tokens, width = own.shape
    kept = width // 2
    part = width // PIECES

    def fetch(piece):
        columns = pl.ds(piece * part, part)
        return pltpu.make_async_copy(
            own_ref.at[:, columns], own.at[:, columns], own_sems.at[piece]
        )

    def store(piece):
        start = piece * (part // 2)
        columns = pl.ds(start, part // 2 if piece < PIECES else send.shape[1] - start)
        return pltpu.make_async_copy(
            send.at[:, columns], send_ref.at[:, columns], send_sems.at[piece]
        )

    fetch_key = pltpu.make_async_copy(key_ref, key, own_sems.at[PIECES])
    for piece in range(PIECES):
        fetch(piece).start()
    fetch_key.start()
    total = jnp.zeros((tokens, 128), jnp.float32)
    for piece in range(PIECES):
        fetch(piece).wait()

        def add(i, total):
            block = own[:, pl.ds(pl.multiple_of(piece * part + i * 512, 512), 512)]
            block = block.astype(jnp.float32)
            block = block * block
            return (
                total
                + (block[:, :128] + block[:, 128:256])
                + (block[:, 256:384] + block[:, 384:])
            )

        total = lax.fori_loop(0, part // 512, add, total)
        for k in range(piece * part // 512, (piece + 1) * part // 512):
            columns = slice(k * 256, k * 256 + 256)
            start = pl.multiple_of(k * 512 + (1 - core_ref[0]) * 256, 256)
            send[:, columns] = own[:, pl.ds(start, 256)]
            start = pl.multiple_of(k * 512 + core_ref[0] * 256, 256)
            kept_ref[:, columns] = own[:, pl.ds(start, 256)]
        store(piece).start()
    mean = jnp.sum(total, axis=1, keepdims=True) * (1.0 / width)
    fetch_key.wait()
    scaled = key[...].astype(jnp.float32) * lax.rsqrt(mean + norm_eps)
    scaled_ref[...] = scaled.astype(jnp.bfloat16)
    send[:, kept:] = scaled_ref[...]
    store(PIECES).start()
    for piece in range(PIECES + 1):
        store(piece).wait()


def pair_kernel(core_ref, kept_ref, scaled_ref, got_ref, out_ref, keys, out, out_sems):
    tokens, kept = kept_ref.shape
    core = core_ref[0]

    def store(side_y, pair_y):
        return pltpu.make_async_copy(
            out.at[side_y, :, pair_y], out_ref.at[side_y, :, pair_y], out_sems.at[side_y, pair_y]
        )

    keys[:tokens, :] = scaled_ref[...]
    keys[tokens:, :] = got_ref[:, kept:]
    places_x = [lax.rem(x + 4 - core, 4) for x in range(4)]
    places_z = [lax.rem(z + 8 - core, 8) for z in range(8)]
    sides_x, pairs_x = [side(p) for p in places_x], [p // 2 for p in places_x]
    sides_z, pairs_z = [side(p) for p in places_z], [p // 2 for p in places_z]

    def step(pair_y, carry):
        for member in range(2):
            place_y = pair_y * 2 + member
            side_y = side(place_y)
            row = lax.rem(place_y + core, 8)
            for xh in range(2):
                columns = pl.ds(pl.multiple_of(row * 512 + xh * 256, 256), 256)
                product = lax.dot_general(
                    jnp.concatenate([kept_ref[:, columns], got_ref[:, columns]], axis=0),
                    keys[...],
                    (((0,), (0,)), ((), ())),
                    preferred_element_type=jnp.float32,
                )
                product = product.astype(jnp.bfloat16).reshape(8, 2, 16, 512)
                for z in range(8):
                    for xl in range(2):
                        x = xh * 2 + xl
                        near = sides_x[x] * 2 + sides_z[z]
                        far = pairs_x[x] * 4 + pairs_z[z]
                        out[side_y, near, pair_y, far] = product[z, xl]
            store(side_y, pair_y).start()
        return carry

    lax.fori_loop(0, 4, step, 0)
    for pair_y in range(4):
        for side_y in range(2):
            store(side_y, pair_y).wait()


SMEM = pl.BlockSpec(memory_space=pltpu.MemorySpace.SMEM)
HBM = pl.BlockSpec(memory_space=pltpu.MemorySpace.HBM)
VMEM = pl.BlockSpec(memory_space=pltpu.MemorySpace.VMEM)


def own_part(core, own, key):
    tokens, width = own.shape
    sent = (tokens, width // 2 + key.shape[1])
    return pl.pallas_call(
        own_kernel,
        in_specs=[SMEM, HBM, HBM],
        out_specs=[HBM, VMEM, VMEM],
        out_shape=[
            jax.ShapeDtypeStruct(sent, jnp.bfloat16),
            jax.ShapeDtypeStruct((tokens, width // 2), jnp.bfloat16),
            jax.ShapeDtypeStruct(key.shape, jnp.bfloat16),
        ],
        scratch_shapes=[
            pltpu.VMEM(own.shape, jnp.bfloat16),
            pltpu.VMEM(key.shape, jnp.bfloat16),
            pltpu.VMEM(sent, jnp.bfloat16),
            pltpu.SemaphoreType.DMA((PIECES + 1,)),
            pltpu.SemaphoreType.DMA((PIECES + 1,)),
        ],
        compiler_params=pltpu.CompilerParams(vmem_limit_bytes=50 * 1024 * 1024),
        cost_estimate=pl.CostEstimate(
            flops=4 * tokens * width, bytes_accessed=5 * 1024 * 1024, transcendentals=0
        ),
    )(core, own, key)


def pair_partial(core, kept, scaled, got):
    tokens, width = kept.shape
    proj = scaled.shape[1]
    shape = (2, 4, 4, 8, 16, proj)
    return pl.pallas_call(
        pair_kernel,
        in_specs=[SMEM, VMEM, VMEM, VMEM],
        out_specs=HBM,
        out_shape=jax.ShapeDtypeStruct(shape, jnp.bfloat16),
        scratch_shapes=[
            pltpu.VMEM((2 * tokens, proj), jnp.bfloat16),
            pltpu.VMEM(shape, jnp.bfloat16),
            pltpu.SemaphoreType.DMA((2, 4)),
        ],
        compiler_params=pltpu.CompilerParams(vmem_limit_bytes=48 * 1024 * 1024),
        cost_estimate=pl.CostEstimate(
            flops=4 * tokens * width * proj, bytes_accessed=9 * 1024 * 1024, transcendentals=0
        ),
    )(core, kept, scaled, got)


def sum_kernel(value_ref, out_ref, out, out_sems):
    sources, blocks = value_ref.shape[:2]
    part = blocks // PIECES

    def store(piece):
        place = pl.ds(piece * part, part)
        return pltpu.make_async_copy(out.at[place], out_ref.at[place], out_sems.at[piece])

    for piece in range(PIECES):

        def add(i, carry):
            place = piece * part + i
            total = value_ref[0, place].astype(jnp.float32)
            for source in range(1, sources):
                total = total + value_ref[source, place].astype(jnp.float32)
            out[place] = total.astype(jnp.bfloat16)
            return carry

        lax.fori_loop(0, part, add, 0)
        store(piece).start()
    for piece in range(PIECES):
        store(piece).wait()


def near_sum(value):
    return pl.pallas_call(
        sum_kernel,
        in_specs=[VMEM],
        out_specs=HBM,
        out_shape=jax.ShapeDtypeStruct(value.shape[1:], jnp.bfloat16),
        scratch_shapes=[
            pltpu.VMEM(value.shape[1:], jnp.bfloat16),
            pltpu.SemaphoreType.DMA((PIECES,)),
        ],
        compiler_params=pltpu.CompilerParams(vmem_limit_bytes=12 * 1024 * 1024),
        cost_estimate=pl.CostEstimate(
            flops=value.size, bytes_accessed=5 * 1024 * 1024, transcendentals=0
        ),
    )(value)


def exchange(value, groups):
    return lax.all_to_all(
        value, ALL, split_axis=0, concat_axis=0, axis_index_groups=groups, tiled=True
    )


def summed(value):
    return jnp.sum(value.astype(jnp.float32), axis=0)


def on_device(
    hidden_in,
    key_grad,
    gain_second,
    weight_second,
    weight_main,
    weight_m,
    weight_v,
    gain_main,
    gain_m,
    gain_v,
):
    y = lax.axis_index(("yh", "yl"))
    target = (lax.axis_index("core") * 8 + lax.rem(y + 4, 8)) * 2 + lax.axis_index("xh")
    rows = lax.dynamic_slice_in_dim(weight_second, target * 16, 16, 0)
    gains = lax.dynamic_slice_in_dim(gain_second, target * 16, 16, 0)
    number = lambda y, xh, core, z, xl: (((y * 2 + xh) * 2 + core) * 8 + z) * 2 + xl
    pairs = [
        (number((z + 4) % 8, xl, core, y, xh), number(y, xh, core, z, xl))
        for y in range(8)
        for xh in range(2)
        for core in range(2)
        for z in range(8)
        for xl in range(2)
    ]
    packed = jnp.concatenate([rows, jnp.broadcast_to(gains[:, None], (16, 128))], axis=1)

    core = lax.axis_index("core").astype(jnp.int32).reshape(1)
    sent, kept, scaled = own_part(core, hidden_in, key_grad)
    got = lax.ppermute(sent, "core", [(0, 1), (1, 0)])
    packed = lax.ppermute(packed, ALL, pairs)
    partial_value = pair_partial(core, kept, scaled, got)
    near_groups, far_groups = exchange_groups()
    near = exchange(partial_value.reshape(8, 32, 16, 512), near_groups)
    scaled_grad = summed(exchange(near_sum(near), far_groups))

    packed = packed.astype(jnp.float32)
    rows, gains = packed[:, :512], packed[:, 512:513]
    weight_grad = scaled_grad * gains
    gain_grad = jnp.sum(scaled_grad * rows, axis=1)
    weight_new, weight_first, weight_square = adam_update(
        weight_main, weight_m, weight_v, weight_grad
    )
    gain_new, gain_first, gain_square = adam_update(gain_main, gain_m, gain_v, gain_grad)
    return (weight_new, weight_first, weight_square, gain_new, gain_first, gain_square)


def solution(mesh):
    fine = Mesh(mesh.devices.reshape(SIZES), ALL)
    placed = (
        P(ALL, None),
        P(ALL, None),
        P(GROUP),
        P(GROUP, None),
        P(ALL, None),
        P(ALL, None),
        P(ALL, None),
        P(ALL),
        P(ALL),
        P(ALL),
    )
    return jax.shard_map(
        on_device,
        mesh=fine,
        in_specs=placed,
        out_specs=(P(ALL, None),) * 3 + (P(ALL),) * 3,
        check_vma=False,
    )
```
